32 devices in a mesh: parts: 2 (over x), seq: 16 (over z, y, core).
Axes of the slice: x: 2, y: 2, z: 4, core: 2. Of those that a mesh axis runs over, the one named last changes fastest.
Arguments:
- pore_features: bfloat16 [12288, 1024], P(('parts', 'seq')), parts along dimension 0, may hold values from -21 to 21
- pore_order: int32 [12288], P(('parts', 'seq')), parts along dimension 0, may hold values from 0 to 6143, as said below
- block_lists: int32 [96, 8], P(('parts', 'seq')), parts along dimension 0, may hold values from 0 to 47, as said below
- block_counts: int32 [96], P(('parts', 'seq')), parts along dimension 0, may hold values from 3 to 8
- norm1_gain: float32 [1024], replicated, may hold values from 0.5 to 1.5
- w_qkv: bfloat16 [1024, 3072], replicated, may hold values from -0.1875 to 0.1875
- query_gain: float32 [64], replicated, may hold values from 0.25 to 1.75
- key_gain: float32 [64], replicated, may hold values from 0.25 to 1.75
- w_attn_out: bfloat16 [1024, 1024], replicated, may hold values from -0.1875 to 0.1875
- norm2_gain: float32 [1024], replicated, may hold values from 0.5 to 1.5
- w_in: bfloat16 [4096, 1024], P('seq'), may hold values from -0.1875 to 0.1875
- w_out: bfloat16 [4096, 1024], P('seq'), may hold values from -0.09375 to 0.09375
Outputs:
- attended: bfloat16 [12288, 1024], P(('parts', 'seq')), parts along dimension 0
- layer_output: bfloat16 [12288, 1024], P(('parts', 'seq')), parts along dimension 0
The draws below stay inside these ranges and needn't reach their ends.
There are 2 independent parts, one for each index of `parts`. The reference program is written for one: setup_inputs(seed, part) draws one part's arguments, and reference() takes and returns one part's arrays. A program takes and returns all parts, laid end to end along the dimension named above; an argument that names none is the same for every part. Nothing has to cross between parts.
Inputs may be any that keep to these rules, and one draw needn't show every extreme that they name: `pore_order`: for every k, entries k * 384 to (k + 1) * 384 - 1 are a permutation of those same numbers. block_lists[b, 0] = b; block_lists[b, 1] is a block of the next lower seq index and block_lists[b, 2] one of the next higher seq index along the closed cycle; the entries of a row are distinct; the seq index of a block c is c // 3, and every listed block lies at most 2 seq indices from that of b along the closed cycle of 16 indices.
All inputs are finite; a program needn't handle non-finite values.
Results may differ from the reference program's by a relative error of at most 0.0057.
Values may be sent and summed in bfloat16 or wider, within the bound.
No kernel may reach another device: no remote copies, remote signals or barrier semaphores. Data moves between devices by JAX's collectives and lax.ppermute only.
A program may use at most 128 MiB of HBM per device.

```python
import math
import jax
import jax.numpy as jnp
from jax import lax

D = 1024
HEADS = 16
FF = 4096
TOK_DEV = 384
BLOCK = 128
REACH = 2
MAXNZ = 8
HEAD_DIM = 64
BLK_DEV = 3
TOKENS = 6144
NBLK = 48
N_SEQ = 16


def draw_pore_features(key, part):
    row_key, col_key, base_key = jax.random.split(key, 3)
    row_scale = jnp.exp(jax.random.uniform(row_key, (TOKENS, 1), jnp.float32, math.log(0.3), math.log(3.0)))
    col_scale = jnp.exp(jax.random.uniform(col_key, (1, D), jnp.float32, math.log(0.5), math.log(2.0)))
    base_values = jnp.clip(jax.random.normal(base_key, (TOKENS, D), jnp.float32), -3.5, 3.5)
    return (base_values * row_scale * col_scale).astype(jnp.bfloat16)


def draw_pore_order(key, part):
    segments = TOKENS // TOK_DEV

    def one_segment(segment_index):
        shuffled = jax.random.permutation(jax.random.fold_in(key, segment_index), TOK_DEV)
        return shuffled.astype(jnp.int32) + segment_index * TOK_DEV
    return jax.vmap(one_segment)(jnp.arange(segments, dtype=jnp.int32)).reshape(TOKENS).astype(jnp.int32)


def draw_block_lists(key, part):
    key = jax.random.fold_in(key, 11)
    window_blocks = (2 * REACH + 1) * BLK_DEV

    def one_block(block_index):
        block_key = jax.random.fold_in(key, block_index)
        lower_key, upper_key, rest_key = jax.random.split(block_key, 3)
        centre = REACH * BLK_DEV + block_index % BLK_DEV
        lower_pick = (REACH - 1) * BLK_DEV + jax.random.randint(lower_key, (), 0, BLK_DEV)
        upper_pick = (REACH + 1) * BLK_DEV + jax.random.randint(upper_key, (), 0, BLK_DEV)
        slots = jnp.arange(window_blocks, dtype=jnp.int32)
        excluded = (slots == centre) | (slots == lower_pick) | (slots == upper_pick)
        ranks = jax.random.permutation(rest_key, window_blocks).astype(jnp.int32)
        order = jnp.argsort(ranks + window_blocks * excluded.astype(jnp.int32))
        rest = order[:MAXNZ - 3].astype(jnp.int32)
        window_slots = jnp.concatenate([jnp.reshape(lower_pick, (1,)), jnp.reshape(upper_pick, (1,)), rest]).astype(jnp.int32)
        device_index = block_index // BLK_DEV
        others = ((device_index - REACH) * BLK_DEV + window_slots) % NBLK
        return jnp.concatenate([jnp.reshape(block_index, (1,)), others])
    return jax.vmap(one_block)(jnp.arange(NBLK, dtype=jnp.int32)).astype(jnp.int32)


def draw_block_counts(key, part):
    key = jax.random.fold_in(key, 23)
    level_key, count_key, device_key, slot_key = jax.random.split(key, 4)
    devices = NBLK // BLK_DEV
    levels = jax.random.randint(level_key, (devices, 1), 1, MAXNZ - 1)
    spread_values = jax.random.randint(count_key, (devices, BLK_DEV), 0, MAXNZ - 2)
    counts = 3 + spread_values % levels
    heavy_device = jax.random.randint(device_key, (), 0, devices)
    full_slot = jax.random.randint(slot_key, (), 0, BLK_DEV)
    full_mask = (jnp.arange(devices)[:, None] == heavy_device) & (jnp.arange(BLK_DEV)[None, :] == full_slot)
    return jnp.where(full_mask, MAXNZ, counts).reshape(NBLK).astype(jnp.int32)


def shard_levels(rng, extent, cuts, low, top_value):
    loudness = 1.0
    for axis_at, parts in cuts:
        draws = jax.random.uniform(jax.random.fold_in(jax.random.fold_in(rng, 6), axis_at), (parts,), jnp.float32, low / len(cuts), top_value / len(cuts))
        loudness = loudness * jnp.repeat(jnp.exp(draws), extent[axis_at] // parts).reshape((-1,) + (1,) * (len(extent) - 1 - axis_at))
    return loudness


def bell_draw(own_key, extent, width, limit, pieces=(), kind=jnp.bfloat16):
    entries = width * jax.random.normal(own_key, extent, jnp.float32)
    if pieces:
        entries = entries * shard_levels(own_key, extent, pieces, -0.22, 0.18)
    return jnp.clip(entries, -limit, limit).astype(kind)


def setup_inputs(seed: int = 0, part: int = 0) -> dict:
    arg_keys = jax.random.split(jax.random.key(seed), 13)
    own_keys = jax.random.split(jax.random.fold_in(arg_keys[12], part), 13)
    return {
        "pore_features": draw_pore_features(jax.random.fold_in(jax.random.fold_in(arg_keys[12], part), 71), part),
        "pore_order": draw_pore_order(jax.random.fold_in(jax.random.fold_in(arg_keys[12], part), 71), part),
        "block_lists": draw_block_lists(jax.random.fold_in(jax.random.fold_in(arg_keys[12], part), 71), part),
        "block_counts": draw_block_counts(jax.random.fold_in(jax.random.fold_in(arg_keys[12], part), 71), part),
        "norm1_gain": jnp.clip(1.0 + 0.1 * jax.random.normal(arg_keys[4], (D,), jnp.float32), 0.5, 1.5),
        "w_qkv": bell_draw(arg_keys[5], (D, 3 * D), D ** -0.5, 0.1875),
        "query_gain": jnp.clip(1.0 + 0.15 * jax.random.normal(arg_keys[6], (HEAD_DIM,), jnp.float32), 0.25, 1.75),
        "key_gain": jnp.clip(1.0 + 0.15 * jax.random.normal(arg_keys[7], (HEAD_DIM,), jnp.float32), 0.25, 1.75),
        "w_attn_out": bell_draw(arg_keys[8], (D, D), D ** -0.5, 0.1875),
        "norm2_gain": jnp.clip(1.0 + 0.1 * jax.random.normal(arg_keys[9], (D,), jnp.float32), 0.5, 1.5),
        "w_in": bell_draw(arg_keys[10], (FF, D), D ** -0.5, 0.1875, ((0, 16),)),
        "w_out": bell_draw(arg_keys[11], (FF, D), FF ** -0.5, 0.09375, ((0, 16),)),
    }


def rms_scale(values, gain):
    widened = values.astype(jnp.float32)
    factor = lax.rsqrt(lax.optimization_barrier(jnp.mean(widened * widened, axis=-1, keepdims=True)) + 1e-06)
    return (widened * factor * gain).astype(jnp.bfloat16)

def head_norm(values, gain, factor_scale):
    shaped = values.reshape(values.shape[0], HEADS, values.shape[1] // HEADS)
    factor = lax.rsqrt(lax.optimization_barrier(jnp.mean(shaped * shaped, axis=-1, keepdims=True)) + 1e-06)
    return (shaped * factor * gain * factor_scale).astype(jnp.bfloat16)

def widen(values):
    return lax.optimization_barrier(values).astype(jnp.float32)

def reference(pore_features, pore_order, block_lists, block_counts, norm1_gain, w_qkv, query_gain, key_gain, w_attn_out, norm2_gain, w_in, w_out):
    ordered = jnp.take(pore_features, pore_order, axis=0)
    normed = rms_scale(ordered, norm1_gain)
    projected = jnp.dot(normed, w_qkv, preferred_element_type=jnp.float32)
    queries = head_norm(projected[:, :D], query_gain, 2.0 / math.sqrt(HEAD_DIM))
    keys = head_norm(projected[:, D:2 * D], key_gain, 1.0)
    values = projected[:, 2 * D:].astype(jnp.bfloat16).reshape(TOKENS, HEADS, HEAD_DIM)
    key_blocks = keys.reshape(NBLK, BLOCK, HEADS, HEAD_DIM)
    value_blocks = values.reshape(NBLK, BLOCK, HEADS, HEAD_DIM)
    query_blocks = queries.reshape(NBLK, BLOCK, HEADS, HEAD_DIM)
    slot_of_key = (jnp.arange(MAXNZ * BLOCK) // BLOCK).astype(jnp.int32)

    def one_block(inputs):
        query_rows, chosen, count_here = inputs
        key_rows = jnp.take(key_blocks, chosen, axis=0).reshape(MAXNZ * BLOCK, HEADS, HEAD_DIM)
        value_rows = jnp.take(value_blocks, chosen, axis=0).reshape(MAXNZ * BLOCK, HEADS, HEAD_DIM)
        scores = jnp.einsum('qhd,khd->hqk', widen(query_rows), widen(key_rows))
        keep_mask = (slot_of_key < count_here)[None, None, :]
        weights = jnp.where(keep_mask, jnp.exp(scores), jnp.zeros_like(scores))
        totals = lax.optimization_barrier(jnp.sum(weights, axis=-1))
        summed = jnp.einsum('hqk,khd->qhd', widen(weights.astype(jnp.bfloat16)), widen(value_rows))
        return (summed / jnp.transpose(totals)[:, :, None]).astype(jnp.bfloat16)
    attention = lax.map(one_block, (query_blocks, block_lists, block_counts)).reshape(TOKENS, D)
    attn_proj = jnp.dot(attention, w_attn_out, preferred_element_type=jnp.float32)
    attended = (ordered.astype(jnp.float32) + attn_proj).astype(jnp.bfloat16)
    second = rms_scale(attended, norm2_gain)

    def one_slab(rows_in):
        pre_act = lax.dot_general(rows_in, w_in, (((1,), (1,)), ((), ())), preferred_element_type=jnp.float32)
        active = jax.nn.gelu(pre_act, approximate=True).astype(jnp.bfloat16)
        return jnp.dot(active, w_out, preferred_element_type=jnp.float32)
    feed_forward = lax.map(one_slab, second.reshape(N_SEQ, TOK_DEV, D)).reshape(TOKENS, D)
    layer_output = (attended.astype(jnp.float32) + feed_forward).astype(jnp.bfloat16)
    return (attended, layer_output)
```

```python
import functools
import math

import jax
import jax.numpy as jnp
from jax import lax
from jax.experimental import pallas as pl
from jax.experimental.pallas import tpu as pltpu
from jax.sharding import PartitionSpec as P

HEADS = 16
BLOCK = 128
REACH = 2
MAXNZ = 8
EPS = 1e-06
MIB = 1024 * 1024


def chip_grid(chips):
    columns = 1 << ((chips.bit_length() - 1) // 2)
    return chips // columns, columns


def chip_cycle(chips):
    rows, columns = chip_grid(chips)
    if columns < 2 or rows % 2:
        return list(range(chips))
    order = [(row, 0) for row in range(rows)]
    for row in reversed(range(rows)):
        inner = list(range(1, columns))
        order += [(row, column) for column in (inner if (rows - 1 - row) % 2 == 0 else inner[::-1])]
    return [row * columns + column for row, column in order]


def prep_kernel(features, order, gain, ordered, normed):
    rows = features.shape[0]
    place = lax.broadcasted_iota(jnp.int32, (rows, rows), 0)
    chosen = (place == order[...]).astype(jnp.bfloat16)
    picked = lax.dot_general(
        chosen, features[...], (((0,), (0,)), ((), ())), preferred_element_type=jnp.float32
    )
    ordered[...] = picked.astype(jnp.bfloat16)
    factor = lax.rsqrt(jnp.mean(picked * picked, axis=-1, keepdims=True) + EPS)
    normed[...] = (picked * factor * gain[...]).astype(jnp.bfloat16)


def prepare(features, order, gain):
    rows, width = features.shape
    shape = jax.ShapeDtypeStruct((rows, width), jnp.bfloat16)
    return pl.pallas_call(
        prep_kernel,
        out_shape=(shape, shape),
        compiler_params=pltpu.CompilerParams(vmem_limit_bytes=24 * MIB),
        cost_estimate=pl.CostEstimate(
            flops=2 * rows * rows * width, bytes_accessed=6 * rows * width, transcendentals=rows
        ),
        name="prepare",
    )(features, order.reshape(1, rows), gain.reshape(1, width))


def head_scale(values, head_dim, gain):
    columns = values.shape[1]
    row = lax.broadcasted_iota(jnp.int32, (columns, columns), 0) // head_dim
    column = lax.broadcasted_iota(jnp.int32, (columns, columns), 1) // head_dim
    same = (row == column).astype(jnp.bfloat16)
    sums = jnp.dot(
        (values * values).astype(jnp.bfloat16), same, preferred_element_type=jnp.float32
    )
    factor = lax.rsqrt(sums * (1.0 / head_dim) + EPS)
    return (values * factor * gain).astype(jnp.bfloat16)


def project_kernel(
    tiles, head_dim, scale, own, mate, weights, query_gain, key_gain, queries, keys, values
):
    step = pl.program_id(0)
    rows = own.shape[0]
    block = weights[...]

    @pl.when(step < tiles)
    def _():
        found = jnp.dot(own[...], block, preferred_element_type=jnp.float32)
        queries[...] = head_scale(found, head_dim, query_gain[...] * scale)

    @pl.when((step >= tiles) & (step < 2 * tiles))
    def _():
        for at, source in enumerate((own, mate)):
            found = jnp.dot(source[...], block, preferred_element_type=jnp.float32)
            keys[at * rows : (at + 1) * rows, :] = head_scale(found, head_dim, key_gain[...])

    @pl.when(step >= 2 * tiles)
    def _():
        for at, source in enumerate((own, mate)):
            found = jnp.dot(source[...], block, preferred_element_type=jnp.float32)
            values[at * rows : (at + 1) * rows, :] = found.astype(jnp.bfloat16)


def project_own(own, mate, weights, query_gain, key_gain, window_rows):
    rows, width = own.shape
    head_dim = query_gain.shape[0]
    columns = 4 * head_dim
    tiles = width // columns
    window = jax.ShapeDtypeStruct((window_rows, width), jnp.bfloat16)
    whole = pl.BlockSpec((rows, width), lambda i: (0, 0))
    gain = pl.BlockSpec((1, columns), lambda i: (0, 0))
    return pl.pallas_call(
        functools.partial(project_kernel, tiles, head_dim, 2.0 / math.sqrt(head_dim)),
        out_shape=(jax.ShapeDtypeStruct((rows, width), jnp.bfloat16), window, window),
        grid=(3 * tiles,),
        in_specs=[whole, whole, pl.BlockSpec((width, columns), lambda i: (0, i)), gain, gain],
        out_specs=(
            pl.BlockSpec((rows, columns), lambda i: (0, jnp.minimum(i, tiles - 1))),
            pl.BlockSpec((2 * rows, columns), lambda i: (0, jnp.clip(i - tiles, 0, tiles - 1))),
            pl.BlockSpec((2 * rows, columns), lambda i: (0, jnp.maximum(i - 2 * tiles, 0))),
        ),
        compiler_params=pltpu.CompilerParams(vmem_limit_bytes=24 * MIB),
        cost_estimate=pl.CostEstimate(
            flops=10 * rows * width * width,
            bytes_accessed=6 * width * width + 14 * rows * width,
            transcendentals=3 * rows * width,
        ),
        name="project_own",
    )(own, mate, weights, jnp.tile(query_gain, 4)[None], jnp.tile(key_gain, 4)[None])


def window_kernel(tiles, head_dim, count, *refs):
    sources = refs[:count]
    weights, key_gain, _, _, keys, values = refs[count:]
    step = pl.program_id(0)
    rows = sources[0].shape[0]
    block = weights[...]

    @pl.when(step < tiles)
    def _():
        for at, source in enumerate(sources):
            found = jnp.dot(source[...], block, preferred_element_type=jnp.float32)
            keys[at * rows : (at + 1) * rows, :] = head_scale(found, head_dim, key_gain[...])

    @pl.when(step >= tiles)
    def _():
        for at, source in enumerate(sources):
            found = jnp.dot(source[...], block, preferred_element_type=jnp.float32)
            values[at * rows : (at + 1) * rows, :] = found.astype(jnp.bfloat16)


def project_window(sources, first, weights, key_gain, keys, values):
    count = len(sources)
    rows, width = sources[0].shape
    head_dim = key_gain.shape[0]
    columns = 4 * head_dim
    tiles = width // columns
    at = first // count
    window = jax.ShapeDtypeStruct(keys.shape, jnp.bfloat16)
    anywhere = pl.BlockSpec(memory_space=pl.ANY)
    return pl.pallas_call(
        functools.partial(window_kernel, tiles, head_dim, count),
        out_shape=(window, window),
        grid=(2 * tiles,),
        in_specs=[pl.BlockSpec((rows, width), lambda i: (0, 0))] * count
        + [
            pl.BlockSpec((width, columns), lambda i: (0, i + tiles)),
            pl.BlockSpec((1, columns), lambda i: (0, 0)),
            anywhere,
            anywhere,
        ],
        out_specs=(
            pl.BlockSpec((count * rows, columns), lambda i: (at, jnp.minimum(i, tiles - 1))),
            pl.BlockSpec((count * rows, columns), lambda i: (at, jnp.maximum(i - tiles, 0))),
        ),
        input_output_aliases={count + 2: 0, count + 3: 1},
        compiler_params=pltpu.CompilerParams(vmem_limit_bytes=24 * MIB),
        cost_estimate=pl.CostEstimate(
            flops=4 * count * rows * width * width,
            bytes_accessed=4 * width * width + 6 * count * rows * width,
            transcendentals=count * rows * width,
        ),
        name="project_window",
    )(*sources, weights, jnp.tile(key_gain, 4)[None], keys, values)


def attend_kernel(
    axis, cycle, lists, counts, queries, keys, values, ordered, weights, gain, attended, second,
    sums, mixed,
):
    rows, width = queries.shape
    blocks = rows // BLOCK
    pairs = sums.shape[0]
    pair = width // pairs
    me = lax.axis_index(axis)
    side = 1 - 2 * lax.rem(me, 2)
    window_blocks = keys.shape[0] // BLOCK
    lane = lax.broadcasted_iota(jnp.int32, (BLOCK, pair), 1)
    low = lane < pair // 2
    key_lane = lax.broadcasted_iota(jnp.int32, (2 * BLOCK, 2 * BLOCK), 1)
    ones = jnp.ones((2 * BLOCK, pair), jnp.bfloat16)

    def place(block):
        holder = lax.div(block, blocks)
        away = lax.rem(holder - me + REACH + cycle, cycle) - REACH
        turned = away * side
        slot = jnp.where(turned > 0, 2 * turned - 1, -2 * turned)
        found = slot * blocks + lax.rem(block, blocks)
        return pl.multiple_of(jnp.clip(found, 0, window_blocks - 1) * BLOCK, BLOCK)

    for at in range(blocks):
        count = counts[at]
        here = pl.ds(at * BLOCK, BLOCK)

        def two_blocks(step, carry, at=at, count=count, here=here):
            one = pl.ds(place(lists[at, 2 * step]), BLOCK)
            other = pl.ds(place(lists[at, 2 * step + 1]), BLOCK)
            limit = jnp.where(2 * step + 1 < count, 2 * BLOCK, BLOCK)
            kept = key_lane < limit
            for index in range(pairs):
                columns = pl.ds(index * pair, pair)
                asked = queries[here, columns]
                none = jnp.zeros_like(asked)
                both = jnp.concatenate(
                    [jnp.where(low, asked, none), jnp.where(low, none, asked)], axis=0
                )
                known = jnp.concatenate([keys[one, columns], keys[other, columns]], axis=0)
                held = jnp.concatenate([values[one, columns], values[other, columns]], axis=0)
                scores = lax.dot_general(
                    both, known, (((1,), (1,)), ((), ())), preferred_element_type=jnp.float32
                )
                shares = jnp.where(kept, jnp.exp(scores), 0.0).astype(jnp.bfloat16)
                found = jnp.dot(
                    shares,
                    jnp.concatenate([held, ones], axis=1),
                    preferred_element_type=jnp.float32,
                )
                sums[index] = jnp.where(step == 0, found, sums[index] + found)
            return carry

        lax.fori_loop(0, lax.div(count + 1, 2), two_blocks, 0)
        for index in range(pairs):
            total = sums[index]
            share = total[:, :pair] / total[:, pair:]
            mixed[here, pl.ds(index * pair, pair)] = jnp.where(
                low, share[:BLOCK], share[BLOCK:]
            ).astype(jnp.bfloat16)

    product = jnp.dot(mixed[...], weights[...], preferred_element_type=jnp.float32)
    result = (ordered[...].astype(jnp.float32) + product).astype(jnp.bfloat16)
    attended[...] = result
    widened = result.astype(jnp.float32)
    factor = lax.rsqrt(jnp.mean(widened * widened, axis=-1, keepdims=True) + EPS)
    second[...] = (widened * factor * gain[...]).astype(jnp.bfloat16)


def attend(axis, cycle, lists, counts, queries, keys, values, ordered, weights, gain):
    rows, width = queries.shape
    shape = jax.ShapeDtypeStruct((rows, width), jnp.bfloat16)
    scalars = pl.BlockSpec(memory_space=pltpu.SMEM)
    local = pl.BlockSpec(memory_space=pltpu.VMEM)
    pairs = width // BLOCK
    work = 2 * rows * MAXNZ * BLOCK * width
    return pl.pallas_call(
        functools.partial(attend_kernel, axis, cycle),
        out_shape=(shape, shape),
        in_specs=[scalars, scalars] + [local] * 6,
        out_specs=(local, local),
        scratch_shapes=[
            pltpu.VMEM((pairs, 2 * BLOCK, 2 * BLOCK), jnp.float32),
            pltpu.VMEM((rows, width), jnp.bfloat16),
        ],
        compiler_params=pltpu.CompilerParams(vmem_limit_bytes=40 * MIB),
        cost_estimate=pl.CostEstimate(
            flops=4 * work + 2 * rows * width * width,
            bytes_accessed=4 * keys.size + 8 * rows * width + 2 * width * width,
            transcendentals=rows * MAXNZ * BLOCK * HEADS,
        ),
        name="attend",
    )(lists, counts, queries, keys, values, ordered, weights, gain.reshape(1, width))


def feed_kernel(steps, second, first_rows, second_rows, attended, result, total):
    step = pl.program_id(0)
    before = lax.dot_general(
        second[...], first_rows[...], (((1,), (1,)), ((), ())), preferred_element_type=jnp.float32
    )
    active = jax.nn.gelu(before, approximate=True).astype(jnp.bfloat16)
    part = jnp.dot(active, second_rows[...], preferred_element_type=jnp.float32)

    @pl.when(step == 0)
    def _():
        total[...] = part

    @pl.when(step > 0)
    def _():
        total[...] += part

    @pl.when(step == steps - 1)
    def _():
        result[...] = (attended[...].astype(jnp.float32) + total[...]).astype(jnp.bfloat16)


def feed_forward(second, first_rows, second_rows, attended):
    rows, width = second.shape
    hidden = first_rows.shape[0]
    chunk = min(512, hidden)
    steps = hidden // chunk
    whole = pl.BlockSpec((rows, width), lambda i: (0, 0))
    part = pl.BlockSpec((chunk, width), lambda i: (i, 0))
    return pl.pallas_call(
        functools.partial(feed_kernel, steps),
        out_shape=jax.ShapeDtypeStruct((rows, width), jnp.bfloat16),
        grid=(steps,),
        in_specs=[whole, part, part, whole],
        out_specs=whole,
        scratch_shapes=[pltpu.VMEM((rows, width), jnp.float32)],
        compiler_params=pltpu.CompilerParams(vmem_limit_bytes=40 * MIB),
        cost_estimate=pl.CostEstimate(
            flops=4 * rows * width * hidden,
            bytes_accessed=4 * hidden * width + 6 * rows * width,
            transcendentals=rows * hidden,
        ),
        name="feed_forward",
    )(second, first_rows, second_rows, attended)


def shards(
    pore_features,
    pore_order,
    block_lists,
    block_counts,
    norm1_gain,
    w_qkv,
    query_gain,
    key_gain,
    w_attn_out,
    norm2_gain,
    w_in,
    w_out,
):
    rows = pore_features.shape[0]
    cycle = lax.axis_size("seq")
    me = lax.axis_index("seq")

    def moved(value, where):
        return lax.ppermute(value, "seq", [(i, where(i) % cycle) for i in range(cycle)])

    def mate_of(value):
        return moved(value, lambda i: i + 1 - 2 * (i % 2))

    ring = [2 * chip + core for chip in chip_cycle(cycle // 2) for core in range(2)]
    gathered_in = lax.all_gather(w_in, "seq", axis=0, tiled=True, axis_index_groups=[ring])
    gathered_out = lax.all_gather(w_out, "seq", axis=0, tiled=True, axis_index_groups=[ring])

    ordered, normed = prepare(pore_features, pore_order - me * rows, norm1_gain)
    near = moved(normed, lambda i: i - 1 + 2 * (i % 2))
    far = moved(normed, lambda i: i + 2 - 4 * (i % 2))
    mate = mate_of(normed)
    queries, keys, values = project_own(
        normed, mate, w_qkv, query_gain, key_gain, (2 * REACH + 1) * rows
    )
    across = mate_of(near)
    keys, values = project_window([near, across], 2, w_qkv, key_gain, keys, values)
    keys, values = project_window([far], 4, w_qkv, key_gain, keys, values)
    attended, second = attend(
        "seq", cycle, block_lists, block_counts, queries, keys, values, ordered, w_attn_out,
        norm2_gain,
    )
    layer_output = feed_forward(second, gathered_in, gathered_out, attended)
    return (attended, layer_output)


def solution(mesh):
    return jax.shard_map(
        shards,
        mesh=mesh,
        in_specs=(
            P(("parts", "seq"), None),
            P(("parts", "seq")),
            P(("parts", "seq"), None),
            P(("parts", "seq")),
            P(),
            P(),
            P(),
            P(),
            P(),
            P(),
            P("seq", None),
            P("seq", None),
        ),
        out_specs=(P(("parts", "seq"), None), P(("parts", "seq"), None)),
        check_vma=False,
    )
```

```python
import functools
import math

import jax
import jax.numpy as jnp
from jax import lax
from jax.experimental import pallas as pl
from jax.experimental.pallas import tpu as pltpu
from jax.sharding import PartitionSpec as P

HEADS = 16
BLOCK = 128
REACH = 2
MAXNZ = 8
EPS = 1e-06
MIB = 1024 * 1024


def chip_grid(chips):
    columns = 1 << ((chips.bit_length() - 1) // 2)
    return chips // columns, columns


def chip_cycle(chips):
    rows, columns = chip_grid(chips)
    if columns < 2 or rows % 2:
        return list(range(chips))
    order = [(row, 0) for row in range(rows)]
    for row in reversed(range(rows)):
        inner = list(range(1, columns))
        order += [(row, column) for column in (inner if (rows - 1 - row) % 2 == 0 else inner[::-1])]
    return [row * columns + column for row, column in order]


def prep_kernel(features, order, gain, ordered, normed):
    rows = features.shape[0]
    place = lax.broadcasted_iota(jnp.int32, (rows, rows), 0)
    chosen = (place == order[...]).astype(jnp.bfloat16)
    picked = lax.dot_general(
        chosen, features[...], (((0,), (0,)), ((), ())), preferred_element_type=jnp.float32
    )
    ordered[...] = picked.astype(jnp.bfloat16)
    factor = lax.rsqrt(jnp.mean(picked * picked, axis=-1, keepdims=True) + EPS)
    normed[...] = (picked * factor * gain[...]).astype(jnp.bfloat16)


def prepare(features, order, gain):
    rows, width = features.shape
    shape = jax.ShapeDtypeStruct((rows, width), jnp.bfloat16)
    return pl.pallas_call(
        prep_kernel,
        out_shape=(shape, shape),
        compiler_params=pltpu.CompilerParams(vmem_limit_bytes=24 * MIB),
        cost_estimate=pl.CostEstimate(
            flops=2 * rows * rows * width, bytes_accessed=6 * rows * width, transcendentals=rows
        ),
        name="prepare",
    )(features, order.reshape(1, rows), gain.reshape(1, width))


def head_scale(values, head_dim, gain):
    columns = values.shape[1]
    row = lax.broadcasted_iota(jnp.int32, (columns, columns), 0) // head_dim
    column = lax.broadcasted_iota(jnp.int32, (columns, columns), 1) // head_dim
    same = (row == column).astype(jnp.bfloat16)
    sums = jnp.dot(
        (values * values).astype(jnp.bfloat16), same, preferred_element_type=jnp.float32
    )
    factor = lax.rsqrt(sums * (1.0 / head_dim) + EPS)
    return (values * factor * gain).astype(jnp.bfloat16)


def project_kernel(tiles, head_dim, scale, source, weights, query_gain, key_gain, *outs):
    step = pl.program_id(0)
    queries, key_values = outs if len(outs) == 2 else (None, outs[0])
    first = tiles if queries is not None else 0
    found = jnp.dot(source[...], weights[...], preferred_element_type=jnp.float32)

    if queries is not None:

        @pl.when(step < tiles)
        def _():
            queries[...] = head_scale(found, head_dim, query_gain[...] * scale)

    @pl.when((step >= first) & (step < first + tiles))
    def _():
        key_values[...] = head_scale(found, head_dim, key_gain[...])

    @pl.when(step >= first + tiles)
    def _():
        key_values[...] = found.astype(jnp.bfloat16)


def project(source, weights, query_gain, key_gain, with_queries):
    rows, width = source.shape
    head_dim = query_gain.shape[0]
    columns = 4 * head_dim
    tiles = width // columns
    skipped = 0 if with_queries else tiles
    steps = 3 * tiles - skipped
    gain = pl.BlockSpec((1, columns), lambda i: (0, 0))
    shapes = [jax.ShapeDtypeStruct((rows, 2 * width), jnp.bfloat16)]
    specs = [pl.BlockSpec((rows, columns), lambda i: (0, jnp.maximum(i - tiles + skipped, 0)))]
    if with_queries:
        shapes.insert(0, jax.ShapeDtypeStruct((rows, width), jnp.bfloat16))
        specs.insert(0, pl.BlockSpec((rows, columns), lambda i: (0, jnp.minimum(i, tiles - 1))))
    return pl.pallas_call(
        functools.partial(project_kernel, tiles, head_dim, 2.0 / math.sqrt(head_dim)),
        out_shape=shapes,
        grid=(steps,),
        in_specs=[
            pl.BlockSpec((rows, width), lambda i: (0, 0)),
            pl.BlockSpec((width, columns), lambda i: (0, i + skipped)),
            gain,
            gain,
        ],
        out_specs=specs,
        compiler_params=pltpu.CompilerParams(vmem_limit_bytes=16 * MIB),
        cost_estimate=pl.CostEstimate(
            flops=2 * rows * width * columns * steps,
            bytes_accessed=2 * width * columns * steps + 8 * rows * width,
            transcendentals=rows * width,
        ),
        name="project",
    )(source, weights, jnp.tile(query_gain, 4)[None], jnp.tile(key_gain, 4)[None])


def attend_kernel(
    axis, cycle, lists, counts, queries, own, mate, near, across, far, ordered, weights, gain,
    attended, second, sums, mixed, window, arrived,
):
    rows, width = queries.shape
    copies = [
        pltpu.make_async_copy(source, window.at[pl.ds(slot * rows, rows)], arrived.at[slot])
        for slot, source in enumerate((own, mate, near, across, far))
    ]
    for copy in copies:
        copy.start()
    for copy in copies:
        copy.wait()
    blocks = rows // BLOCK
    pairs = sums.shape[0]
    pair = width // pairs
    me = lax.axis_index(axis)
    side = 1 - 2 * lax.rem(me, 2)
    window_blocks = window.shape[0] // BLOCK
    lane = lax.broadcasted_iota(jnp.int32, (BLOCK, pair), 1)
    low = lane < pair // 2
    key_lane = lax.broadcasted_iota(jnp.int32, (2 * BLOCK, 2 * BLOCK), 1)
    ones = jnp.ones((2 * BLOCK, pair), jnp.bfloat16)

    def place(block):
        holder = lax.div(block, blocks)
        away = lax.rem(holder - me + REACH + cycle, cycle) - REACH
        turned = away * side
        slot = jnp.where(turned > 0, 2 * turned - 1, -2 * turned)
        found = slot * blocks + lax.rem(block, blocks)
        return pl.multiple_of(jnp.clip(found, 0, window_blocks - 1) * BLOCK, BLOCK)

    for at in range(blocks):
        count = counts[at]
        here = pl.ds(at * BLOCK, BLOCK)

        def two_blocks(step, carry, at=at, count=count, here=here):
            one = pl.ds(place(lists[at, 2 * step]), BLOCK)
            other = pl.ds(place(lists[at, 2 * step + 1]), BLOCK)
            limit = jnp.where(2 * step + 1 < count, 2 * BLOCK, BLOCK)
            kept = key_lane < limit
            for index in range(pairs):
                columns = pl.ds(index * pair, pair)
                asked = queries[here, columns]
                none = jnp.zeros_like(asked)
                both = jnp.concatenate(
                    [jnp.where(low, asked, none), jnp.where(low, none, asked)], axis=0
                )
                known = jnp.concatenate([window[one, columns], window[other, columns]], axis=0)
                later = pl.ds(width + index * pair, pair)
                held = jnp.concatenate([window[one, later], window[other, later]], axis=0)
                scores = lax.dot_general(
                    both, known, (((1,), (1,)), ((), ())), preferred_element_type=jnp.float32
                )
                shares = jnp.where(kept, jnp.exp(scores), 0.0).astype(jnp.bfloat16)
                found = jnp.dot(
                    shares,
                    jnp.concatenate([held, ones], axis=1),
                    preferred_element_type=jnp.float32,
                )
                sums[index] = jnp.where(step == 0, found, sums[index] + found)
            return carry

        lax.fori_loop(0, lax.div(count + 1, 2), two_blocks, 0)
        for index in range(pairs):
            total = sums[index]
            share = total[:, :pair] / total[:, pair:]
            mixed[here, pl.ds(index * pair, pair)] = jnp.where(
                low, share[:BLOCK], share[BLOCK:]
            ).astype(jnp.bfloat16)

    product = jnp.dot(mixed[...], weights[...], preferred_element_type=jnp.float32)
    result = (ordered[...].astype(jnp.float32) + product).astype(jnp.bfloat16)
    attended[...] = result
    widened = result.astype(jnp.float32)
    factor = lax.rsqrt(jnp.mean(widened * widened, axis=-1, keepdims=True) + EPS)
    second[...] = (widened * factor * gain[...]).astype(jnp.bfloat16)


def attend(axis, cycle, lists, counts, queries, sources, ordered, weights, gain):
    rows, width = queries.shape
    shape = jax.ShapeDtypeStruct((rows, width), jnp.bfloat16)
    scalars = pl.BlockSpec(memory_space=pltpu.SMEM)
    local = pl.BlockSpec(memory_space=pltpu.VMEM)
    anywhere = pl.BlockSpec(memory_space=pl.ANY)
    pairs = width // BLOCK
    slots = len(sources)
    work = 2 * rows * MAXNZ * BLOCK * width
    return pl.pallas_call(
        functools.partial(attend_kernel, axis, cycle),
        out_shape=(shape, shape),
        in_specs=[scalars, scalars, local] + [anywhere] * slots + [local] * 3,
        out_specs=(local, local),
        scratch_shapes=[
            pltpu.VMEM((pairs, 2 * BLOCK, 2 * BLOCK), jnp.float32),
            pltpu.VMEM((rows, width), jnp.bfloat16),
            pltpu.VMEM((slots * rows, 2 * width), jnp.bfloat16),
            pltpu.SemaphoreType.DMA((slots,)),
        ],
        compiler_params=pltpu.CompilerParams(vmem_limit_bytes=32 * MIB),
        cost_estimate=pl.CostEstimate(
            flops=4 * work + 2 * rows * width * width,
            bytes_accessed=4 * slots * rows * width + 8 * rows * width + 2 * width * width,
            transcendentals=rows * MAXNZ * BLOCK * HEADS,
        ),
        name="attend",
    )(lists, counts, queries, *sources, ordered, weights, gain.reshape(1, width))


def pieces_kernel(axis, swaps, has_base, *refs):
    count = len(swaps)
    second = refs[0]
    firsts = refs[1 : 1 + count]
    seconds = refs[1 + count : 1 + 2 * count]
    base = refs[1 + 2 * count] if has_base else None
    result = refs[-1]
    straight = lax.axis_index(axis) == 0
    rows = second[...]
    total = base[...] if has_base else None
    for index, swapped in enumerate(swaps):
        first_rows, second_rows = firsts[index][...], seconds[index][...]
        if swapped:
            first_rows, second_rows = (
                jnp.where(straight, first_rows, second_rows),
                jnp.where(straight, second_rows, first_rows),
            )
        before = lax.dot_general(
            rows, first_rows, (((1,), (1,)), ((), ())), preferred_element_type=jnp.float32
        )
        active = jax.nn.gelu(before, approximate=True).astype(jnp.bfloat16)
        part = jnp.dot(active, second_rows, preferred_element_type=jnp.float32)
        total = part if total is None else total + part
    result[...] = total.astype(result.dtype)


def feed_pieces(axis, second, pieces, base, dtype):
    rows, width = second.shape
    hidden = sum(piece[0].shape[0] for piece in pieces)
    operands = [second] + [piece[0] for piece in pieces] + [piece[1] for piece in pieces]
    if base is not None:
        operands.append(base)
    local = pl.BlockSpec(memory_space=pltpu.VMEM)
    return pl.pallas_call(
        functools.partial(
            pieces_kernel, axis, tuple(piece[2] for piece in pieces), base is not None
        ),
        out_shape=jax.ShapeDtypeStruct((rows, width), dtype),
        in_specs=[local] * len(operands),
        out_specs=local,
        compiler_params=pltpu.CompilerParams(vmem_limit_bytes=32 * MIB),
        cost_estimate=pl.CostEstimate(
            flops=4 * rows * width * hidden,
            bytes_accessed=4 * hidden * width + 8 * rows * width,
            transcendentals=rows * hidden,
        ),
        name="feed_pieces",
    )(*operands)


def feed_kernel(steps, second, first_rows, second_rows, attended, result, total):
    step = pl.program_id(0)
    before = lax.dot_general(
        second[...], first_rows[...], (((1,), (1,)), ((), ())), preferred_element_type=jnp.float32
    )
    active = jax.nn.gelu(before, approximate=True).astype(jnp.bfloat16)
    part = jnp.dot(active, second_rows[...], preferred_element_type=jnp.float32)

    @pl.when(step == 0)
    def _():
        total[...] = part

    @pl.when(step > 0)
    def _():
        total[...] += part

    @pl.when(step == steps - 1)
    def _():
        result[...] = (attended[...].astype(jnp.float32) + total[...]).astype(jnp.bfloat16)


def feed_forward(second, first_rows, second_rows, attended):
    rows, width = second.shape
    hidden = first_rows.shape[0]
    chunk = min(512, hidden)
    steps = hidden // chunk
    whole = pl.BlockSpec((rows, width), lambda i: (0, 0))
    part = pl.BlockSpec((chunk, width), lambda i: (i, 0))
    return pl.pallas_call(
        functools.partial(feed_kernel, steps),
        out_shape=jax.ShapeDtypeStruct((rows, width), jnp.bfloat16),
        grid=(steps,),
        in_specs=[whole, part, part, whole],
        out_specs=whole,
        scratch_shapes=[pltpu.VMEM((rows, width), jnp.float32)],
        compiler_params=pltpu.CompilerParams(vmem_limit_bytes=40 * MIB),
        cost_estimate=pl.CostEstimate(
            flops=4 * rows * width * hidden,
            bytes_accessed=4 * hidden * width + 6 * rows * width,
            transcendentals=rows * hidden,
        ),
        name="feed_forward",
    )(second, first_rows, second_rows, attended)


def shards(
    pore_features,
    pore_order,
    block_lists,
    block_counts,
    norm1_gain,
    w_qkv,
    query_gain,
    key_gain,
    w_attn_out,
    norm2_gain,
    w_in,
    w_out,
):
    rows = pore_features.shape[0]
    cycle = lax.axis_size("seq")
    me = lax.axis_index("seq")

    def moved(value, where):
        return lax.ppermute(value, "seq", [(i, where(i) % cycle) for i in range(cycle)])

    def mate_of(value):
        return moved(value, lambda i: i + 1 - 2 * (i % 2))

    chip_rows, chip_columns = chip_grid(cycle // 2)
    shared = (chip_rows, chip_columns) == (4, 2) and lax.axis_size("parts") == 2
    lane = 2 * chip_columns

    def along(value, targets):
        pairs = [(lane * a + k, lane * b + k) for a, b in targets for k in range(lane)]
        return lax.ppermute(value, "seq", pairs)

    def beside(value):
        return moved(value, lambda i: i + 2 - 4 * (i // 2 % 2))

    def over(value):
        return lax.ppermute(value, "parts", [(0, 1), (1, 0)])

    ordered, normed = prepare(pore_features, pore_order - me * rows, norm1_gain)
    near = moved(normed, lambda i: i - 1 + 2 * (i % 2))
    far = moved(normed, lambda i: i + 2 - 4 * (i % 2))

    if shared:
        row = me // lane
        inner = (row == 1) | (row == 2)
        prime = jnp.where(lax.axis_index("parts") == 0, w_in, w_out)
        pair_rows = along(prime, [(0, 1), (1, 0), (2, 3), (3, 2)])
        inner_own = along(prime, [(1, 2), (2, 1)])
        inner_pair = along(pair_rows, [(1, 2), (2, 1)])
        outer_own = along(inner_own, [(1, 0), (2, 3)])
        outer_pair = along(inner_pair, [(1, 0), (2, 3)])
        third = jnp.where(inner, inner_own, outer_own)
        fourth = jnp.where(inner, inner_pair, outer_pair)
        pieces = [(w_in, w_out, False), (mate_of(w_in), mate_of(w_out), False)]
        for prime_rows in (pair_rows, third, fourth):
            other_rows = over(prime_rows)
            pieces.append((prime_rows, other_rows, True))
            pieces.append((mate_of(prime_rows), mate_of(other_rows), True))

    queries, own_kv = project(normed, w_qkv, query_gain, key_gain, True)
    mate_kv = mate_of(own_kv)
    (near_kv,) = project(near, w_qkv, query_gain, key_gain, False)
    across_kv = mate_of(near_kv)
    (far_kv,) = project(far, w_qkv, query_gain, key_gain, False)
    attended, second = attend(
        "seq", cycle, block_lists, block_counts, queries,
        [own_kv, mate_kv, near_kv, across_kv, far_kv], ordered, w_attn_out, norm2_gain,
    )
    if shared:
        guest = beside(second)
        early = feed_pieces("parts", second, pieces[:6], None, jnp.float32)
        guest_part = feed_pieces("parts", guest, pieces, None, jnp.bfloat16)
        returned = beside(guest_part)
        own_part = feed_pieces("parts", second, pieces[6:], early, jnp.float32)
        layer_output = (
            attended.astype(jnp.float32) + own_part + returned.astype(jnp.float32)
        ).astype(jnp.bfloat16)
    else:
        ring = [2 * chip + core for chip in chip_cycle(cycle // 2) for core in range(2)]
        gathered_in = lax.all_gather(w_in, "seq", axis=0, tiled=True, axis_index_groups=[ring])
        gathered_out = lax.all_gather(w_out, "seq", axis=0, tiled=True, axis_index_groups=[ring])
        layer_output = feed_forward(second, gathered_in, gathered_out, attended)
    return (attended, layer_output)


def solution(mesh):
    return jax.shard_map(
        shards,
        mesh=mesh,
        in_specs=(
            P(("parts", "seq"), None),
            P(("parts", "seq")),
            P(("parts", "seq"), None),
            P(("parts", "seq")),
            P(),
            P(),
            P(),
            P(),
            P(),
            P(),
            P("seq", None),
            P("seq", None),
        ),
        out_specs=(P(("parts", "seq"), None), P(("parts", "seq"), None)),
        check_vma=False,
    )
```

```python
import functools
import math

import jax
import jax.numpy as jnp
from jax import lax
from jax.experimental import pallas as pl
from jax.experimental.pallas import tpu as pltpu
from jax.sharding import PartitionSpec as P

HEADS = 16
BLOCK = 128
REACH = 2
MAXNZ = 8
EPS = 1e-06
ATTEND_COST = 10**9
MIB = 1024 * 1024


def chip_grid(chips):
    columns = 1 << ((chips.bit_length() - 1) // 2)
    return chips // columns, columns


def chip_cycle(chips):
    rows, columns = chip_grid(chips)
    if columns < 2 or rows % 2:
        return list(range(chips))
    order = [(row, 0) for row in range(rows)]
    for row in reversed(range(rows)):
        inner = list(range(1, columns))
        order += [(row, column) for column in (inner if (rows - 1 - row) % 2 == 0 else inner[::-1])]
    return [row * columns + column for row, column in order]


def cost(flops, moved, part=64):
    return pl.CostEstimate(flops=flops // part, bytes_accessed=moved // part, transcendentals=0)


def ordered_rows(axis, features, order):
    rows = features.shape[0]
    place = lax.broadcasted_iota(jnp.int32, (rows, rows), 0) + lax.axis_index(axis) * rows
    chosen = (place == order[...]).astype(jnp.bfloat16)
    return lax.dot_general(
        chosen, features[...], (((0,), (0,)), ((), ())), preferred_element_type=jnp.float32
    )


def norm_kernel(axis, features, order, gain, normed):
    picked = ordered_rows(axis, features, order)
    factor = lax.rsqrt(jnp.mean(picked * picked, axis=-1, keepdims=True) + EPS)
    normed[...] = (picked * factor * gain[...]).astype(jnp.bfloat16)


def order_kernel(axis, features, order, ordered):
    ordered[...] = ordered_rows(axis, features, order).astype(jnp.bfloat16)


def prepare(features, order, gain=None):
    rows, width = features.shape
    operands = [features, order.reshape(1, rows)]
    if gain is not None:
        operands.append(gain.reshape(1, width))
    return pl.pallas_call(
        functools.partial(order_kernel if gain is None else norm_kernel, "seq"),
        out_shape=jax.ShapeDtypeStruct((rows, width), jnp.bfloat16),
        compiler_params=pltpu.CompilerParams(vmem_limit_bytes=16 * MIB),
        cost_estimate=cost(2 * rows * rows * width, 6 * rows * width),
        name="order" if gain is None else "norm",
    )(*operands)


def choose_kernel(axis, one, other, chosen):
    @pl.when(lax.axis_index(axis) == 0)
    def _():
        chosen[...] = one[...]

    @pl.when(lax.axis_index(axis) != 0)
    def _():
        chosen[...] = other[...]


def choose(axis, one, other):
    return pl.pallas_call(
        functools.partial(choose_kernel, axis),
        out_shape=jax.ShapeDtypeStruct(one.shape, one.dtype),
        compiler_params=pltpu.CompilerParams(vmem_limit_bytes=16 * MIB),
        cost_estimate=cost(0, 6 * one.size),
        name="choose",
    )(one, other)


def head_scale(values, head_dim, gain):
    columns = values.shape[1]
    row = lax.broadcasted_iota(jnp.int32, (columns, columns), 0) // head_dim
    column = lax.broadcasted_iota(jnp.int32, (columns, columns), 1) // head_dim
    same = (row == column).astype(jnp.bfloat16)
    sums = jnp.dot(
        (values * values).astype(jnp.bfloat16), same, preferred_element_type=jnp.float32
    )
    factor = lax.rsqrt(sums * (1.0 / head_dim) + EPS)
    return (values * factor * gain).astype(jnp.bfloat16)


def project_into(source, weights, first, head_dim, scaled, out):
    width = source.shape[1]
    chunk = 4 * head_dim
    at = 0
    for columns, gain in scaled:
        for _ in range(columns // chunk):
            found = jnp.dot(
                source, weights[:, first + at : first + at + chunk],
                preferred_element_type=jnp.float32,
            )
            out(at, found.astype(jnp.bfloat16) if gain is None else head_scale(found, head_dim, gain))
            at += chunk


def project_into(source, weights, first, head_dim, scaled, out):
    width = source.shape[1]
    chunk = 4 * head_dim
    at = 0
    for columns, gain in scaled:
        for _ in range(columns // chunk):
            found = jnp.dot(
                source, weights[:, first + at : first + at + chunk],
                preferred_element_type=jnp.float32,
            )
            out(at, found.astype(jnp.bfloat16) if gain is None else head_scale(found, head_dim, gain))
            at += chunk


def project_kernel(head_dim, scale, count, with_queries, *refs):
    sources = refs[:count]
    weights, query_gain, key_gain, *rest = refs[count:]
    queries = rest[0] if with_queries else None
    key_values, gathered = rest[-2:]
    width = sources[0].shape[1]
    chunk = 4 * head_dim
    at = 0
    for source in sources:
        gathered[at : at + source.shape[0], :] = source[...]
        at += source.shape[0]

    def store_key_value(at, value):
        key_values[:, at : at + chunk] = value

    def store_query(at, value):
        queries[:, at : at + chunk] = value

    if with_queries:
        gain = query_gain[...] * scale
        project_into(sources[0][...], weights, 0, head_dim, [(width, gain)], store_query)
    project_into(
        gathered[...], weights, width, head_dim, [(width, key_gain[...]), (width, None)],
        store_key_value,
    )


def project(sources, weights, query_gain, key_gain, with_queries):
    width = sources[0].shape[1]
    rows = sum(source.shape[0] for source in sources)
    head_dim = query_gain.shape[0]
    shapes = [jax.ShapeDtypeStruct((rows, 2 * width), jnp.bfloat16)]
    if with_queries:
        shapes.insert(0, jax.ShapeDtypeStruct(sources[0].shape, jnp.bfloat16))
    local = pl.BlockSpec(memory_space=pltpu.VMEM)
    return pl.pallas_call(
        functools.partial(
            project_kernel, head_dim, 2.0 / math.sqrt(head_dim), len(sources), with_queries
        ),
        out_shape=shapes,
        in_specs=[local] * (len(sources) + 3),
        out_specs=[local] * len(shapes),
        scratch_shapes=[pltpu.VMEM((rows, width), jnp.bfloat16)],
        compiler_params=pltpu.CompilerParams(vmem_limit_bytes=24 * MIB),
        cost_estimate=cost(4 * rows * width * width, 8 * width * width),
        name="project",
    )(*sources, weights, jnp.tile(query_gain, 4)[None], jnp.tile(key_gain, 4)[None])


def slot_of(block, me, cycle, blocks):
    holder = lax.div(block, blocks)
    away = lax.rem(holder - me + REACH + cycle, cycle) - REACH
    turned = away * (1 - 2 * lax.rem(me, 2))
    return jnp.where(turned > 0, 2 * turned - 1, -2 * turned), lax.rem(block, blocks)


def pick_blocks(lists, counts, picks, at, me, cycle, blocks, wanted):
    found = 0
    count = counts[at]
    for index in range(MAXNZ):
        slot, place = slot_of(lists[at, index], me, cycle, blocks)
        take = (index < count) & wanted(slot)
        spot = found

        @pl.when(take)
        def _(slot=slot, place=place, spot=spot):
            picks[spot] = slot * blocks + place

        found = found + take.astype(jnp.int32)

    @pl.when(lax.rem(found, 2) == 1)
    def _(found=found):
        picks[found] = picks[found - 1]

    return found


def add_blocks(queries, window, picks, sums, here, count):
    width = queries.shape[1]
    pairs = sums.shape[0]
    pair = width // pairs
    low = lax.broadcasted_iota(jnp.int32, (BLOCK, pair), 1) < pair // 2
    key_lane = lax.broadcasted_iota(jnp.int32, (2 * BLOCK, 2 * BLOCK), 1)
    ones = jnp.ones((2 * BLOCK, pair), jnp.bfloat16)

    def two_blocks(step, carry):
        one = pl.ds(pl.multiple_of(picks[2 * step] * BLOCK, BLOCK), BLOCK)
        other = pl.ds(pl.multiple_of(picks[2 * step + 1] * BLOCK, BLOCK), BLOCK)
        kept = key_lane < jnp.where(2 * step + 1 < count, 2 * BLOCK, BLOCK)
        for index in range(pairs):
            columns = pl.ds(index * pair, pair)
            later = pl.ds(width + index * pair, pair)
            asked = queries[here, columns]
            none = jnp.zeros_like(asked)
            both = jnp.concatenate(
                [jnp.where(low, asked, none), jnp.where(low, none, asked)], axis=0
            )
            known = jnp.concatenate([window[one, columns], window[other, columns]], axis=0)
            held = jnp.concatenate([window[one, later], window[other, later]], axis=0)
            scores = lax.dot_general(
                both, known, (((1,), (1,)), ((), ())), preferred_element_type=jnp.float32
            )
            shares = jnp.where(kept, jnp.exp(scores), 0.0).astype(jnp.bfloat16)
            found = jnp.dot(
                shares, jnp.concatenate([held, ones], axis=1), preferred_element_type=jnp.float32
            )
            sums[index] = jnp.where(step == 0, found, sums[index] + found)
        return carry

    lax.fori_loop(0, lax.div(count + 1, 2), two_blocks, 0)


def attend_kernel(
    axis, cycle, lists, counts, queries, own_mate, near_across, mixed, totals,
    sums, window, picks,
):
    rows, width = queries.shape
    blocks = rows // BLOCK
    pairs = sums.shape[0]
    pair = width // pairs
    me = lax.axis_index(axis)
    low = lax.broadcasted_iota(jnp.int32, (BLOCK, pair), 1) < pair // 2
    window[: 2 * rows, :] = own_mate[...]
    window[2 * rows :, :] = near_across[...]
    for at in range(blocks):
        here = pl.ds(at * BLOCK, BLOCK)
        count = pick_blocks(
            lists, counts, picks, at, me, cycle, blocks, lambda slot: slot < 2 * REACH
        )
        add_blocks(queries, window, picks, sums, here, count)
        for index in range(pairs):
            total = sums[index]
            columns = pl.ds(index * pair, pair)
            mixed[here, columns] = jnp.where(low, total[:BLOCK, :pair], total[BLOCK:, :pair])
            totals[here, columns] = jnp.where(low, total[:BLOCK, pair:], total[BLOCK:, pair:])


def attend(axis, cycle, lists, counts, queries, sources):
    rows, width = queries.shape
    shape = jax.ShapeDtypeStruct((rows, width), jnp.float32)
    scalars = pl.BlockSpec(memory_space=pltpu.SMEM)
    local = pl.BlockSpec(memory_space=pltpu.VMEM)
    pairs = width // BLOCK
    slots = 2 * REACH
    work = 2 * rows * MAXNZ * BLOCK * width
    return pl.pallas_call(
        functools.partial(attend_kernel, axis, cycle),
        out_shape=(shape, shape),
        in_specs=[scalars, scalars, local] + [local] * len(sources),
        out_specs=(local, local),
        scratch_shapes=[
            pltpu.VMEM((pairs, 2 * BLOCK, 2 * BLOCK), jnp.float32),
            pltpu.VMEM((slots * rows, 2 * width), jnp.bfloat16),
            pltpu.SMEM((MAXNZ,), jnp.int32),
        ],
        compiler_params=pltpu.CompilerParams(vmem_limit_bytes=32 * MIB),
        cost_estimate=pl.CostEstimate(
            flops=ATTEND_COST, bytes_accessed=4 * slots * rows * width, transcendentals=0
        ),
        name="attend",
    )(lists, counts, queries, *sources)


def finish_kernel(
    axis, cycle, head_dim, lists, counts, queries, far, qkv_weights, key_gain, mixed, totals,
    attention, sums, window, picks,
):
    rows, width = queries.shape
    blocks = rows // BLOCK
    pairs = sums.shape[0]
    pair = width // pairs
    chunk = 4 * head_dim
    me = lax.axis_index(axis)
    low = lax.broadcasted_iota(jnp.int32, (BLOCK, pair), 1) < pair // 2

    def store(at, value):
        window[:, at : at + chunk] = value

    project_into(
        far[...], qkv_weights, width, head_dim, [(width, key_gain[...]), (width, None)], store
    )
    for at in range(blocks):
        here = pl.ds(at * BLOCK, BLOCK)
        count = pick_blocks(
            lists, counts, picks, at, me, cycle, blocks, lambda slot: slot == 2 * REACH
        )
        shift = 2 * REACH * blocks

        @pl.when(count == 0)
        def _():
            sums[...] = jnp.zeros_like(sums)

        for index in range(blocks + 1):
            picks[index] = jnp.clip(picks[index] - shift, 0, blocks - 1)
        add_blocks(queries, window, picks, sums, here, count)
        for index in range(pairs):
            total = sums[index]
            columns = pl.ds(index * pair, pair)
            share = (
                mixed[here, columns] + jnp.where(low, total[:BLOCK, :pair], total[BLOCK:, :pair])
            ) / (
                totals[here, columns] + jnp.where(low, total[:BLOCK, pair:], total[BLOCK:, pair:])
            )
            attention[here, columns] = share.astype(jnp.bfloat16)


def finish(
    axis, cycle, lists, counts, queries, far, qkv_weights, key_gain, mixed, totals,
):
    rows, width = queries.shape
    head_dim = key_gain.shape[0]
    shape = jax.ShapeDtypeStruct((rows, width), jnp.bfloat16)
    scalars = pl.BlockSpec(memory_space=pltpu.SMEM)
    local = pl.BlockSpec(memory_space=pltpu.VMEM)
    pairs = width // BLOCK
    return pl.pallas_call(
        functools.partial(finish_kernel, axis, cycle, head_dim),
        out_shape=shape,
        in_specs=[scalars, scalars] + [local] * 6,
        out_specs=local,
        scratch_shapes=[
            pltpu.VMEM((pairs, 2 * BLOCK, 2 * BLOCK), jnp.float32),
            pltpu.VMEM((rows, 2 * width), jnp.bfloat16),
            pltpu.SMEM((MAXNZ,), jnp.int32),
        ],
        compiler_params=pltpu.CompilerParams(vmem_limit_bytes=32 * MIB),
        cost_estimate=cost(6 * rows * width * width, 8 * width * width),
        name="finish",
    )(
        lists, counts, queries, far, qkv_weights, jnp.tile(key_gain, 4)[None], mixed, totals
    )


def output_kernel(attention, ordered, weights, gain, attended, *seconds):
    product = jnp.dot(attention[...], weights[...], preferred_element_type=jnp.float32)
    result = (ordered[...].astype(jnp.float32) + product).astype(jnp.bfloat16)
    attended[...] = result
    widened = result.astype(jnp.float32)
    factor = lax.rsqrt(jnp.mean(widened * widened, axis=-1, keepdims=True) + EPS)
    second = (widened * factor * gain[...]).astype(jnp.bfloat16)
    part = second.shape[0] // len(seconds)
    for index, kept in enumerate(seconds):
        kept[...] = second[index * part : (index + 1) * part]


def attention_output(attention, ordered, weights, gain, parts):
    rows, width = attention.shape
    shape = jax.ShapeDtypeStruct((rows, width), jnp.bfloat16)
    return pl.pallas_call(
        output_kernel,
        out_shape=[shape] + [jax.ShapeDtypeStruct((rows // parts, width), jnp.bfloat16)] * parts,
        compiler_params=pltpu.CompilerParams(vmem_limit_bytes=24 * MIB),
        cost_estimate=cost(2 * rows * width * width, 2 * width * width),
        name="attention_output",
    )(attention, ordered, weights, gain.reshape(1, width))


def pieces_kernel(axis, swaps, sources, bases, *refs):
    count = len(swaps)
    seconds, refs = refs[:sources], refs[sources:]
    firsts, refs = refs[:count], refs[count:]
    lasts, refs = refs[:count], refs[count:]
    base, results = refs[:bases], refs[bases:]
    straight = lax.axis_index(axis) == 0
    rows = jnp.concatenate([second[...] for second in seconds], axis=0)
    total = None
    for index, swapped in enumerate(swaps):
        first_rows, last_rows = firsts[index][...], lasts[index][...]
        if swapped:
            first_rows, last_rows = (
                jnp.where(straight, first_rows, last_rows),
                jnp.where(straight, last_rows, first_rows),
            )
        before = lax.dot_general(
            rows, first_rows, (((1,), (1,)), ((), ())), preferred_element_type=jnp.float32
        )
        active = jax.nn.gelu(before, approximate=True).astype(jnp.bfloat16)
        part = jnp.dot(active, last_rows, preferred_element_type=jnp.float32)
        total = part if total is None else total + part
    if bases:
        known = jnp.concatenate([part[...] for part in base], axis=0)
        total = total + known.astype(jnp.float32)
    part = total.shape[0] // len(results)
    for index, result in enumerate(results):
        result[...] = total[index * part : (index + 1) * part].astype(result.dtype)


def feed_pieces(axis, seconds, pieces, base, dtype, parts=1):
    rows = sum(second.shape[0] for second in seconds)
    width = seconds[0].shape[1]
    hidden = sum(piece[0].shape[0] for piece in pieces)
    operands = [*seconds] + [piece[0] for piece in pieces] + [piece[1] for piece in pieces]
    return pl.pallas_call(
        functools.partial(
            pieces_kernel, axis, tuple(piece[2] for piece in pieces), len(seconds), len(base)
        ),
        out_shape=[jax.ShapeDtypeStruct((rows // parts, width), dtype)] * parts,
        compiler_params=pltpu.CompilerParams(vmem_limit_bytes=24 * MIB),
        cost_estimate=cost(4 * rows * width * hidden, 4 * hidden * width),
        name="feed_pieces",
    )(*operands, *base)


def total_kernel(attended, own, *refs):
    *returned, result = refs
    part = result.shape[0] // len(returned)
    for index, back in enumerate(returned):
        here = pl.ds(index * part, part)
        result[here, :] = (
            attended[here, :].astype(jnp.float32) + own[here, :] + back[...].astype(jnp.float32)
        ).astype(result.dtype)


def total_of(attended, own, returned):
    return pl.pallas_call(
        total_kernel,
        out_shape=jax.ShapeDtypeStruct(attended.shape, attended.dtype),
        compiler_params=pltpu.CompilerParams(vmem_limit_bytes=16 * MIB),
        cost_estimate=cost(attended.size, 10 * attended.size),
        name="total",
    )(attended, own, *returned)


def feed_kernel(steps, second, first_rows, second_rows, attended, result, total):
    step = pl.program_id(0)
    before = lax.dot_general(
        second[...], first_rows[...], (((1,), (1,)), ((), ())), preferred_element_type=jnp.float32
    )
    active = jax.nn.gelu(before, approximate=True).astype(jnp.bfloat16)
    part = jnp.dot(active, second_rows[...], preferred_element_type=jnp.float32)

    @pl.when(step == 0)
    def _():
        total[...] = part

    @pl.when(step > 0)
    def _():
        total[...] += part

    @pl.when(step == steps - 1)
    def _():
        result[...] = (attended[...].astype(jnp.float32) + total[...]).astype(jnp.bfloat16)


def feed_forward(second, first_rows, second_rows, attended):
    rows, width = second.shape
    hidden = first_rows.shape[0]
    chunk = min(512, hidden)
    steps = hidden // chunk
    whole = pl.BlockSpec((rows, width), lambda i: (0, 0))
    part = pl.BlockSpec((chunk, width), lambda i: (i, 0))
    return pl.pallas_call(
        functools.partial(feed_kernel, steps),
        out_shape=jax.ShapeDtypeStruct((rows, width), jnp.bfloat16),
        grid=(steps,),
        in_specs=[whole, part, part, whole],
        out_specs=whole,
        scratch_shapes=[pltpu.VMEM((rows, width), jnp.float32)],
        compiler_params=pltpu.CompilerParams(vmem_limit_bytes=40 * MIB),
        cost_estimate=pl.CostEstimate(
            flops=4 * rows * width * hidden,
            bytes_accessed=4 * hidden * width + 6 * rows * width,
            transcendentals=rows * hidden,
        ),
        name="feed_forward",
    )(second, first_rows, second_rows, attended)


def shards(
    pore_features,
    pore_order,
    block_lists,
    block_counts,
    norm1_gain,
    w_qkv,
    query_gain,
    key_gain,
    w_attn_out,
    norm2_gain,
    w_in,
    w_out,
):
    rows = pore_features.shape[0]
    cycle = lax.axis_size("seq")
    me = lax.axis_index("seq")

    def moved(value, where):
        return lax.ppermute(value, "seq", [(i, where(i) % cycle) for i in range(cycle)])

    def mate_of(value):
        return moved(value, lambda i: i + 1 - 2 * (i % 2))

    chip_rows, chip_columns = chip_grid(cycle // 2)
    shared = (chip_rows, chip_columns) == (4, 2) and lax.axis_size("parts") == 2
    lane = 2 * chip_columns

    def along(value, targets):
        pairs = [(lane * a + k, lane * b + k) for a, b in targets for k in range(lane)]
        return lax.ppermute(value, "seq", pairs)

    def beside(value):
        return moved(value, lambda i: i + 2 - 4 * (i // 2 % 2))

    def over(value):
        return lax.ppermute(value, "parts", [(0, 1), (1, 0)])

    normed = prepare(pore_features, pore_order, norm1_gain)
    near = moved(normed, lambda i: i - 1 + 2 * (i % 2))
    mate = mate_of(normed)
    queries, own_mate = project([normed, mate], w_qkv, query_gain, key_gain, True)
    queries, near, late_normed, late_features = lax.optimization_barrier(
        (queries, near, normed, pore_features)
    )
    far = moved(late_normed, lambda i: i + 2 - 4 * (i % 2))
    ordered = prepare(late_features, pore_order)
    across = [mate_of(part) for part in jnp.split(near, 4)]

    if shared:
        swap = [(0, 1), (1, 0), (2, 3), (3, 2)]
        prime = choose("parts", w_in, w_out)
        pair_rows = along(prime, swap)
        third = along(prime, [(0, 2), (1, 3), (2, 0), (3, 1)])
    (near_across,) = project([near, *across], w_qkv, query_gain, key_gain, False)
    mixed, totals = attend(
        "seq", cycle, block_lists, block_counts, queries, [own_mate, near_across]
    )
    if shared:
        mixed, totals, third, pair_rows = lax.optimization_barrier(
            (mixed, totals, third, pair_rows)
        )
        other_pair = over(pair_rows)
        fourth = along(third, swap)
        other_third = over(third)
        mixed, totals, far = lax.optimization_barrier((mixed, totals, far))
    attention = finish(
        "seq", cycle, block_lists, block_counts, queries, far, w_qkv, key_gain, mixed, totals
    )
    if shared:
        attention, other_pair = lax.optimization_barrier((attention, other_pair))
    parts = 2 if shared else 1
    attended, *seconds = attention_output(attention, ordered, w_attn_out, norm2_gain, parts)
    if shared:
        guests = [beside(second) for second in seconds]
        mate_seconds = [mate_of(second) for second in seconds]
        attended, fourth = lax.optimization_barrier((attended, fourth))
        other_fourth = over(fourth)
        pieces = [
            (w_in, w_out, False),
            (pair_rows, other_pair, True),
            (third, other_third, True),
            (fourth, other_fourth, True),
        ]
        returned = []
        for guest in guests:
            (guest_mate_part,) = feed_pieces("parts", [mate_of(guest)], pieces, [], jnp.bfloat16)
            (guest_part,) = feed_pieces(
                "parts", [guest], pieces, [mate_of(guest_mate_part)], jnp.bfloat16
            )
            returned.append(beside(guest_part))
        returned[0], *mate_seconds = lax.optimization_barrier((returned[0], *mate_seconds))
        mate_parts = feed_pieces("parts", mate_seconds, pieces, [], jnp.bfloat16, 4)
        (own_part,) = feed_pieces(
            "parts", seconds, pieces, [mate_of(part) for part in mate_parts], jnp.float32
        )
        layer_output = total_of(attended, own_part, returned)
    else:
        ring = [2 * chip + core for chip in chip_cycle(cycle // 2) for core in range(2)]
        gathered_in = lax.all_gather(w_in, "seq", axis=0, tiled=True, axis_index_groups=[ring])
        gathered_out = lax.all_gather(w_out, "seq", axis=0, tiled=True, axis_index_groups=[ring])
        layer_output = feed_forward(seconds[0], gathered_in, gathered_out, attended)
    return (attended, layer_output)


def solution(mesh):
    return jax.shard_map(
        shards,
        mesh=mesh,
        in_specs=(
            P(("parts", "seq"), None),
            P(("parts", "seq")),
            P(("parts", "seq"), None),
            P(("parts", "seq")),
            P(),
            P(),
            P(),
            P(),
            P(),
            P(),
            P("seq", None),
            P("seq", None),
        ),
        out_specs=(P(("parts", "seq"), None), P(("parts", "seq"), None)),
        check_vma=False,
    )
```

```python
import functools
import math

import jax
import jax.numpy as jnp
from jax import lax
from jax.experimental import pallas as pl
from jax.experimental.pallas import tpu as pltpu
from jax.sharding import PartitionSpec as P

HEADS = 16
BLOCK = 128
REACH = 2
MAXNZ = 8
EPS = 1e-06
ATTEND_COST = 5 * 10**8
MIB = 1024 * 1024


def chip_grid(chips):
    columns = 1 << ((chips.bit_length() - 1) // 2)
    return chips // columns, columns


def chip_cycle(chips):
    rows, columns = chip_grid(chips)
    if columns < 2 or rows % 2:
        return list(range(chips))
    order = [(row, 0) for row in range(rows)]
    for row in reversed(range(rows)):
        inner = list(range(1, columns))
        order += [(row, column) for column in (inner if (rows - 1 - row) % 2 == 0 else inner[::-1])]
    return [row * columns + column for row, column in order]


def cost(flops, moved, part=64):
    return pl.CostEstimate(flops=flops // part, bytes_accessed=moved // part, transcendentals=0)


def ordered_rows(axis, features, order):
    rows = features.shape[0]
    place = lax.broadcasted_iota(jnp.int32, (rows, rows), 0) + lax.axis_index(axis) * rows
    chosen = (place == order[...]).astype(jnp.bfloat16)
    return lax.dot_general(
        chosen, features[...], (((0,), (0,)), ((), ())), preferred_element_type=jnp.float32
    )


def norm_kernel(axis, features, order, gain, normed, *parts):
    picked = ordered_rows(axis, features, order)
    factor = lax.rsqrt(jnp.mean(picked * picked, axis=-1, keepdims=True) + EPS)
    found = (picked * factor * gain[...]).astype(jnp.bfloat16)
    normed[...] = found
    size = found.shape[0] // len(parts)
    for index, part in enumerate(parts):
        part[...] = found[index * size : (index + 1) * size]


def order_kernel(axis, features, order, ordered):
    ordered[...] = ordered_rows(axis, features, order).astype(jnp.bfloat16)


def prepare(features, order, gain=None):
    rows, width = features.shape
    shapes = [jax.ShapeDtypeStruct((rows, width), jnp.bfloat16)]
    if gain is not None:
        shapes += [jax.ShapeDtypeStruct((rows // 2, width), jnp.bfloat16)] * 2
    operands = [features, order.reshape(1, rows)]
    if gain is not None:
        operands.append(gain.reshape(1, width))
    return pl.pallas_call(
        functools.partial(order_kernel if gain is None else norm_kernel, "seq"),
        out_shape=shapes,
        compiler_params=pltpu.CompilerParams(vmem_limit_bytes=16 * MIB),
        cost_estimate=cost(2 * rows * rows * width, 6 * rows * width),
        name="order" if gain is None else "norm",
    )(*operands)


def choose_kernel(axis, one, other, chosen, left, arrived):
    straight = lax.axis_index(axis) == 0

    def copies(first, second):
        return (
            pltpu.make_async_copy(first, chosen, arrived.at[0]),
            pltpu.make_async_copy(second, left, arrived.at[1]),
        )

    @pl.when(straight)
    def _():
        for copy in copies(one, other):
            copy.start()

    @pl.when(jnp.logical_not(straight))
    def _():
        for copy in copies(other, one):
            copy.start()

    for copy in copies(one, other):
        copy.wait()


def choose(axis, one, other):
    anywhere = pl.BlockSpec(memory_space=pl.ANY)
    local = pl.BlockSpec(memory_space=pltpu.VMEM)
    return pl.pallas_call(
        functools.partial(choose_kernel, axis),
        out_shape=[jax.ShapeDtypeStruct(one.shape, one.dtype)] * 2,
        in_specs=[anywhere, anywhere],
        out_specs=[local, local],
        scratch_shapes=[pltpu.SemaphoreType.DMA((2,))],
        compiler_params=pltpu.CompilerParams(vmem_limit_bytes=60 * MIB),
        cost_estimate=cost(0, 6 * one.size),
        name="choose",
    )(one, other)


def head_scale(values, head_dim, gain):
    columns = values.shape[1]
    row = lax.broadcasted_iota(jnp.int32, (columns, columns), 0) // head_dim
    column = lax.broadcasted_iota(jnp.int32, (columns, columns), 1) // head_dim
    same = (row == column).astype(jnp.bfloat16)
    sums = jnp.dot(
        (values * values).astype(jnp.bfloat16), same, preferred_element_type=jnp.float32
    )
    factor = lax.rsqrt(sums * (1.0 / head_dim) + EPS)
    return (values * factor * gain).astype(jnp.bfloat16)


def project_into(source, weights, first, head_dim, scaled, out):
    width = source.shape[1]
    chunk = 4 * head_dim
    at = 0
    for columns, gain in scaled:
        for _ in range(columns // chunk):
            found = jnp.dot(
                source, weights[:, first + at : first + at + chunk],
                preferred_element_type=jnp.float32,
            )
            out(at, found.astype(jnp.bfloat16) if gain is None else head_scale(found, head_dim, gain))
            at += chunk


def project_into(source, weights, first, head_dim, scaled, out):
    width = source.shape[1]
    chunk = 4 * head_dim
    at = 0
    for columns, gain in scaled:
        for _ in range(columns // chunk):
            found = jnp.dot(
                source, weights[:, first + at : first + at + chunk],
                preferred_element_type=jnp.float32,
            )
            out(at, found.astype(jnp.bfloat16) if gain is None else head_scale(found, head_dim, gain))
            at += chunk


def project_kernel(head_dim, scale, count, with_queries, *refs):
    sources = refs[:count]
    weights, query_gain, key_gain, *rest = refs[count:]
    queries = rest[0] if with_queries else None
    key_values, gathered = rest[-2:]
    width = sources[0].shape[1]
    chunk = 4 * head_dim
    at = 0
    for source in sources:
        gathered[at : at + source.shape[0], :] = source[...]
        at += source.shape[0]

    def store_key_value(at, value):
        key_values[:, at : at + chunk] = value

    def store_query(at, value):
        queries[:, at : at + chunk] = value

    if with_queries:
        gain = query_gain[...] * scale
        project_into(sources[0][...], weights, 0, head_dim, [(width, gain)], store_query)
    project_into(
        gathered[...], weights, width, head_dim, [(width, key_gain[...]), (width, None)],
        store_key_value,
    )


def project(sources, weights, query_gain, key_gain, with_queries):
    width = sources[0].shape[1]
    rows = sum(source.shape[0] for source in sources)
    head_dim = query_gain.shape[0]
    shapes = [jax.ShapeDtypeStruct((rows, 2 * width), jnp.bfloat16)]
    if with_queries:
        shapes.insert(0, jax.ShapeDtypeStruct(sources[0].shape, jnp.bfloat16))
    local = pl.BlockSpec(memory_space=pltpu.VMEM)
    return pl.pallas_call(
        functools.partial(
            project_kernel, head_dim, 2.0 / math.sqrt(head_dim), len(sources), with_queries
        ),
        out_shape=shapes,
        in_specs=[local] * (len(sources) + 3),
        out_specs=[local] * len(shapes),
        scratch_shapes=[pltpu.VMEM((rows, width), jnp.bfloat16)],
        compiler_params=pltpu.CompilerParams(vmem_limit_bytes=24 * MIB),
        cost_estimate=cost(4 * rows * width * width, 8 * width * width),
        name="project",
    )(*sources, weights, jnp.tile(query_gain, 4)[None], jnp.tile(key_gain, 4)[None])


def slot_of(block, me, cycle, blocks):
    holder = lax.div(block, blocks)
    away = lax.rem(holder - me + REACH + cycle, cycle) - REACH
    turned = away * (1 - 2 * lax.rem(me, 2))
    return jnp.where(turned > 0, 2 * turned - 1, -2 * turned), lax.rem(block, blocks)


def pick_blocks(lists, counts, picks, at, me, cycle, blocks, wanted):
    found = 0
    count = counts[at]
    for index in range(MAXNZ):
        slot, place = slot_of(lists[at, index], me, cycle, blocks)
        take = (index < count) & wanted(slot)
        spot = found

        @pl.when(take)
        def _(slot=slot, place=place, spot=spot):
            picks[spot] = slot * blocks + place

        found = found + take.astype(jnp.int32)

    @pl.when(lax.rem(found, 2) == 1)
    def _(found=found):
        picks[found] = picks[found - 1]

    return found


def add_blocks(queries, window, picks, sums, here, count):
    width = queries.shape[1]
    pairs = sums.shape[0]
    pair = width // pairs
    low = lax.broadcasted_iota(jnp.int32, (BLOCK, pair), 1) < pair // 2
    key_lane = lax.broadcasted_iota(jnp.int32, (2 * BLOCK, 2 * BLOCK), 1)
    ones = jnp.ones((2 * BLOCK, pair), jnp.bfloat16)

    def two_blocks(step, carry):
        one = pl.ds(pl.multiple_of(picks[2 * step] * BLOCK, BLOCK), BLOCK)
        other = pl.ds(pl.multiple_of(picks[2 * step + 1] * BLOCK, BLOCK), BLOCK)
        kept = key_lane < jnp.where(2 * step + 1 < count, 2 * BLOCK, BLOCK)
        for index in range(pairs):
            columns = pl.ds(index * pair, pair)
            later = pl.ds(width + index * pair, pair)
            asked = queries[here, columns]
            none = jnp.zeros_like(asked)
            both = jnp.concatenate(
                [jnp.where(low, asked, none), jnp.where(low, none, asked)], axis=0
            )
            known = jnp.concatenate([window[one, columns], window[other, columns]], axis=0)
            held = jnp.concatenate([window[one, later], window[other, later]], axis=0)
            scores = lax.dot_general(
                both, known, (((1,), (1,)), ((), ())), preferred_element_type=jnp.float32
            )
            shares = jnp.where(kept, jnp.exp(scores), 0.0).astype(jnp.bfloat16)
            found = jnp.dot(
                shares, jnp.concatenate([held, ones], axis=1), preferred_element_type=jnp.float32
            )
            sums[index] = jnp.where(step == 0, found, sums[index] + found)
        return carry

    lax.fori_loop(0, lax.div(count + 1, 2), two_blocks, 0)


def attend_kernel(
    axis, cycle, lists, counts, queries, own_mate, near, across, mixed, totals,
    sums, window, picks,
):
    rows, width = queries.shape
    blocks = rows // BLOCK
    pairs = sums.shape[0]
    pair = width // pairs
    me = lax.axis_index(axis)
    low = lax.broadcasted_iota(jnp.int32, (BLOCK, pair), 1) < pair // 2
    window[: 2 * rows, :] = own_mate[...]
    window[2 * rows : 3 * rows, :] = near[...]
    window[3 * rows :, :] = across[...]
    for at in range(blocks):
        here = pl.ds(at * BLOCK, BLOCK)
        count = pick_blocks(
            lists, counts, picks, at, me, cycle, blocks, lambda slot: slot < 2 * REACH
        )
        add_blocks(queries, window, picks, sums, here, count)
        for index in range(pairs):
            total = sums[index]
            columns = pl.ds(index * pair, pair)
            mixed[here, columns] = jnp.where(low, total[:BLOCK, :pair], total[BLOCK:, :pair])
            totals[here, columns] = jnp.where(low, total[:BLOCK, pair:], total[BLOCK:, pair:])


def attend(axis, cycle, lists, counts, queries, sources):
    rows, width = queries.shape
    shape = jax.ShapeDtypeStruct((rows, width), jnp.float32)
    scalars = pl.BlockSpec(memory_space=pltpu.SMEM)
    local = pl.BlockSpec(memory_space=pltpu.VMEM)
    pairs = width // BLOCK
    slots = 2 * REACH
    work = 2 * rows * MAXNZ * BLOCK * width
    return pl.pallas_call(
        functools.partial(attend_kernel, axis, cycle),
        out_shape=(shape, shape),
        in_specs=[scalars, scalars, local] + [local] * len(sources),
        out_specs=(local, local),
        scratch_shapes=[
            pltpu.VMEM((pairs, 2 * BLOCK, 2 * BLOCK), jnp.float32),
            pltpu.VMEM((slots * rows, 2 * width), jnp.bfloat16),
            pltpu.SMEM((MAXNZ,), jnp.int32),
        ],
        compiler_params=pltpu.CompilerParams(vmem_limit_bytes=32 * MIB),
        cost_estimate=pl.CostEstimate(
            flops=ATTEND_COST, bytes_accessed=4 * slots * rows * width, transcendentals=0
        ),
        name="attend",
    )(lists, counts, queries, *sources)


def finish_kernel(
    axis, cycle, lists, counts, queries, window, mixed, totals, attention, sums, picks,
):
    rows, width = queries.shape
    blocks = rows // BLOCK
    pairs = sums.shape[0]
    pair = width // pairs
    me = lax.axis_index(axis)
    low = lax.broadcasted_iota(jnp.int32, (BLOCK, pair), 1) < pair // 2

    for at in range(blocks):
        here = pl.ds(at * BLOCK, BLOCK)
        count = pick_blocks(
            lists, counts, picks, at, me, cycle, blocks, lambda slot: slot == 2 * REACH
        )
        shift = 2 * REACH * blocks

        @pl.when(count == 0)
        def _():
            sums[...] = jnp.zeros_like(sums)

        for index in range(blocks + 1):
            picks[index] = jnp.clip(picks[index] - shift, 0, blocks - 1)
        add_blocks(queries, window, picks, sums, here, count)
        for index in range(pairs):
            total = sums[index]
            columns = pl.ds(index * pair, pair)
            share = (
                mixed[here, columns] + jnp.where(low, total[:BLOCK, :pair], total[BLOCK:, :pair])
            ) / (
                totals[here, columns] + jnp.where(low, total[:BLOCK, pair:], total[BLOCK:, pair:])
            )
            attention[here, columns] = share.astype(jnp.bfloat16)


def finish(
    axis, cycle, lists, counts, queries, far_kv, mixed, totals
):
    rows, width = queries.shape
    shape = jax.ShapeDtypeStruct((rows, width), jnp.bfloat16)
    scalars = pl.BlockSpec(memory_space=pltpu.SMEM)
    local = pl.BlockSpec(memory_space=pltpu.VMEM)
    pairs = width // BLOCK
    return pl.pallas_call(
        functools.partial(finish_kernel, axis, cycle),
        out_shape=shape,
        in_specs=[scalars, scalars] + [local] * 4,
        out_specs=local,
        scratch_shapes=[
            pltpu.VMEM((pairs, 2 * BLOCK, 2 * BLOCK), jnp.float32),
            pltpu.SMEM((MAXNZ,), jnp.int32),
        ],
        compiler_params=pltpu.CompilerParams(vmem_limit_bytes=32 * MIB),
        cost_estimate=cost(6 * rows * width * width, 8 * width * width),
        name="finish",
    )(
        lists, counts, queries, far_kv, mixed, totals
    )


def output_kernel(attention, ordered, weights, gain, attended, *seconds):
    product = jnp.dot(attention[...], weights[...], preferred_element_type=jnp.float32)
    result = (ordered[...].astype(jnp.float32) + product).astype(jnp.bfloat16)
    attended[...] = result
    widened = result.astype(jnp.float32)
    factor = lax.rsqrt(jnp.mean(widened * widened, axis=-1, keepdims=True) + EPS)
    second = (widened * factor * gain[...]).astype(jnp.bfloat16)
    part = second.shape[0] // len(seconds)
    for index, kept in enumerate(seconds):
        kept[...] = second[index * part : (index + 1) * part]


def attention_output(attention, ordered, weights, gain, parts):
    rows, width = attention.shape
    shape = jax.ShapeDtypeStruct((rows, width), jnp.bfloat16)
    return pl.pallas_call(
        output_kernel,
        out_shape=[shape] + [jax.ShapeDtypeStruct((rows // parts, width), jnp.bfloat16)] * parts,
        compiler_params=pltpu.CompilerParams(vmem_limit_bytes=24 * MIB),
        cost_estimate=cost(2 * rows * width * width, 2 * width * width),
        name="attention_output",
    )(attention, ordered, weights, gain.reshape(1, width))


def pieces_kernel(axis, swaps, sources, bases, *refs):
    count = len(swaps)
    seconds, refs = refs[:sources], refs[sources:]
    firsts, refs = refs[:count], refs[count:]
    lasts, refs = refs[:count], refs[count:]
    base, results = refs[:bases], refs[bases:]
    straight = lax.axis_index(axis) == 0
    rows = jnp.concatenate([second[...] for second in seconds], axis=0)
    total = None
    for index, swapped in enumerate(swaps):
        first_rows, last_rows = firsts[index][...], lasts[index][...]
        if swapped:
            first_rows, last_rows = (
                jnp.where(straight, first_rows, last_rows),
                jnp.where(straight, last_rows, first_rows),
            )
        before = lax.dot_general(
            rows, first_rows, (((1,), (1,)), ((), ())), preferred_element_type=jnp.float32
        )
        active = jax.nn.gelu(before, approximate=True).astype(jnp.bfloat16)
        part = jnp.dot(active, last_rows, preferred_element_type=jnp.float32)
        total = part if total is None else total + part
    if bases:
        known = jnp.concatenate([part[...] for part in base], axis=0)
        total = total + known.astype(jnp.float32)
    part = total.shape[0] // len(results)
    for index, result in enumerate(results):
        result[...] = total[index * part : (index + 1) * part].astype(result.dtype)


def feed_pieces(axis, seconds, pieces, base, dtype, parts=1):
    rows = sum(second.shape[0] for second in seconds)
    width = seconds[0].shape[1]
    hidden = sum(piece[0].shape[0] for piece in pieces)
    operands = [*seconds] + [piece[0] for piece in pieces] + [piece[1] for piece in pieces]
    return pl.pallas_call(
        functools.partial(
            pieces_kernel, axis, tuple(piece[2] for piece in pieces), len(seconds), len(base)
        ),
        out_shape=[jax.ShapeDtypeStruct((rows // parts, width), dtype)] * parts,
        compiler_params=pltpu.CompilerParams(vmem_limit_bytes=24 * MIB),
        cost_estimate=cost(4 * rows * width * hidden, 4 * hidden * width),
        name="feed_pieces",
    )(*operands, *base)


def total_kernel(attended, own, *refs):
    *returned, result = refs
    part = result.shape[0] // len(returned)
    for index, back in enumerate(returned):
        here = pl.ds(index * part, part)
        result[here, :] = (
            attended[here, :].astype(jnp.float32) + own[here, :] + back[...].astype(jnp.float32)
        ).astype(result.dtype)


def total_of(attended, own, returned):
    return pl.pallas_call(
        total_kernel,
        out_shape=jax.ShapeDtypeStruct(attended.shape, attended.dtype),
        compiler_params=pltpu.CompilerParams(vmem_limit_bytes=16 * MIB),
        cost_estimate=cost(attended.size, 10 * attended.size),
        name="total",
    )(attended, own, *returned)


def feed_kernel(steps, second, first_rows, second_rows, attended, result, total):
    step = pl.program_id(0)
    before = lax.dot_general(
        second[...], first_rows[...], (((1,), (1,)), ((), ())), preferred_element_type=jnp.float32
    )
    active = jax.nn.gelu(before, approximate=True).astype(jnp.bfloat16)
    part = jnp.dot(active, second_rows[...], preferred_element_type=jnp.float32)

    @pl.when(step == 0)
    def _():
        total[...] = part

    @pl.when(step > 0)
    def _():
        total[...] += part

    @pl.when(step == steps - 1)
    def _():
        result[...] = (attended[...].astype(jnp.float32) + total[...]).astype(jnp.bfloat16)


def feed_forward(second, first_rows, second_rows, attended):
    rows, width = second.shape
    hidden = first_rows.shape[0]
    chunk = min(512, hidden)
    steps = hidden // chunk
    whole = pl.BlockSpec((rows, width), lambda i: (0, 0))
    part = pl.BlockSpec((chunk, width), lambda i: (i, 0))
    return pl.pallas_call(
        functools.partial(feed_kernel, steps),
        out_shape=jax.ShapeDtypeStruct((rows, width), jnp.bfloat16),
        grid=(steps,),
        in_specs=[whole, part, part, whole],
        out_specs=whole,
        scratch_shapes=[pltpu.VMEM((rows, width), jnp.float32)],
        compiler_params=pltpu.CompilerParams(vmem_limit_bytes=40 * MIB),
        cost_estimate=pl.CostEstimate(
            flops=4 * rows * width * hidden,
            bytes_accessed=4 * hidden * width + 6 * rows * width,
            transcendentals=rows * hidden,
        ),
        name="feed_forward",
    )(second, first_rows, second_rows, attended)


def shards(
    pore_features,
    pore_order,
    block_lists,
    block_counts,
    norm1_gain,
    w_qkv,
    query_gain,
    key_gain,
    w_attn_out,
    norm2_gain,
    w_in,
    w_out,
):
    rows = pore_features.shape[0]
    cycle = lax.axis_size("seq")
    me = lax.axis_index("seq")

    def moved(value, where):
        return lax.ppermute(value, "seq", [(i, where(i) % cycle) for i in range(cycle)])

    def mate_of(value):
        return moved(value, lambda i: i + 1 - 2 * (i % 2))

    chip_rows, chip_columns = chip_grid(cycle // 2)
    lane = 2 * chip_columns

    def along(value, targets):
        pairs = [(lane * a + k, lane * b + k) for a, b in targets for k in range(lane)]
        return lax.ppermute(value, "seq", pairs)

    def beside(value):
        return moved(value, lambda i: i + 2 - 4 * (i // 2 % 2))

    def over(value):
        return lax.ppermute(value, "parts", [(0, 1), (1, 0)])

    shared = (chip_rows, chip_columns) == (4, 2) and lax.axis_size("parts") == 2
    if shared:
        swap = [(0, 1), (1, 0), (2, 3), (3, 2)]
        prime, left = choose("parts", w_in, w_out)
        pair_rows = along(prime, swap)
        third = along(prime, [(0, 2), (1, 3), (2, 0), (3, 1)])
    normed, *normed_parts = prepare(pore_features, pore_order, norm1_gain)
    near = [moved(part, lambda i: i - 1 + 2 * (i % 2)) for part in normed_parts]
    mate = mate_of(normed)
    queries, own_mate = project([normed, mate], w_qkv, query_gain, key_gain, True)
    queries, late_normed, late_features, *near = lax.optimization_barrier(
        (queries, normed, pore_features, *near)
    )
    far = moved(late_normed, lambda i: i + 2 - 4 * (i % 2))
    (ordered,) = prepare(late_features, pore_order)
    across = [mate_of(piece) for part in near for piece in jnp.split(part, 2)]

    (near_kv,) = project(near, w_qkv, query_gain, key_gain, False)
    if shared:
        near_kv, *across = lax.optimization_barrier((near_kv, *across))
    (across_kv,) = project(across, w_qkv, query_gain, key_gain, False)
    mixed, totals = attend(
        "seq", cycle, block_lists, block_counts, queries, [own_mate, near_kv, across_kv]
    )
    if shared:
        mixed, totals, third, pair_rows, left = lax.optimization_barrier(
            (mixed, totals, third, pair_rows, left)
        )
        other_pair = along(left, swap)
        fourth = along(third, swap)
        other_third = over(third)
        mixed, totals, far, ordered = lax.optimization_barrier((mixed, totals, far, ordered))
    (far_kv,) = project([far], w_qkv, query_gain, key_gain, False)
    attention = finish(
        "seq", cycle, block_lists, block_counts, queries, far_kv, mixed, totals
    )
    parts = 2 if shared else 1
    attended, *seconds = attention_output(attention, ordered, w_attn_out, norm2_gain, parts)
    if shared:
        guests = [beside(second) for second in seconds]
        mate_seconds = [mate_of(second) for second in seconds]
        attended, fourth = lax.optimization_barrier((attended, fourth))
        guests[0], other_pair, other_third = lax.optimization_barrier(
            (guests[0], other_pair, other_third)
        )
        other_fourth = over(fourth)
        pieces = [
            (w_in, w_out, False),
            (pair_rows, other_pair, True),
            (third, other_third, True),
        ]
        guest_mate_parts = [
            feed_pieces("parts", [mate_of(guest)], pieces, [], jnp.bfloat16)[0] for guest in guests
        ]
        other_fourth, *guest_mate_parts = lax.optimization_barrier(
            (other_fourth, *guest_mate_parts)
        )
        every = [
            *pieces,
            (fourth, other_fourth, True),
            (mate_of(fourth), mate_of(other_fourth), True),
        ]
        returned = []
        for guest, part in zip(guests, guest_mate_parts):
            (guest_part,) = feed_pieces("parts", [guest], every, [mate_of(part)], jnp.bfloat16)
            returned.append(beside(guest_part))
        returned[0], *mate_seconds = lax.optimization_barrier((returned[0], *mate_seconds))
        mate_parts = feed_pieces("parts", mate_seconds, pieces, [], jnp.bfloat16, 4)
        (own_part,) = feed_pieces(
            "parts", seconds, every, [mate_of(part) for part in mate_parts], jnp.float32
        )
        layer_output = total_of(attended, own_part, returned)
    else:
        ring = [2 * chip + core for chip in chip_cycle(cycle // 2) for core in range(2)]
        gathered_in = lax.all_gather(w_in, "seq", axis=0, tiled=True, axis_index_groups=[ring])
        gathered_out = lax.all_gather(w_out, "seq", axis=0, tiled=True, axis_index_groups=[ring])
        layer_output = feed_forward(seconds[0], gathered_in, gathered_out, attended)
    return (attended, layer_output)


def solution(mesh):
    return jax.shard_map(
        shards,
        mesh=mesh,
        in_specs=(
            P(("parts", "seq"), None),
            P(("parts", "seq")),
            P(("parts", "seq"), None),
            P(("parts", "seq")),
            P(),
            P(),
            P(),
            P(),
            P(),
            P(),
            P("seq", None),
            P("seq", None),
        ),
        out_specs=(P(("parts", "seq"), None), P(("parts", "seq"), None)),
        check_vma=False,
    )
```

```python
import functools
import math

import jax
import jax.numpy as jnp
from jax import lax
from jax.experimental import pallas as pl
from jax.experimental.pallas import tpu as pltpu
from jax.sharding import PartitionSpec as P

HEADS = 16
BLOCK = 128
REACH = 2
MAXNZ = 8
EPS = 1e-06
ATTEND_COST = 5 * 10**8
MIB = 1024 * 1024


def chip_grid(chips):
    columns = 1 << ((chips.bit_length() - 1) // 2)
    return chips // columns, columns


def chip_cycle(chips):
    rows, columns = chip_grid(chips)
    if columns < 2 or rows % 2:
        return list(range(chips))
    order = [(row, 0) for row in range(rows)]
    for row in reversed(range(rows)):
        inner = list(range(1, columns))
        order += [(row, column) for column in (inner if (rows - 1 - row) % 2 == 0 else inner[::-1])]
    return [row * columns + column for row, column in order]


def cost(flops, moved, part=64):
    return pl.CostEstimate(flops=flops // part, bytes_accessed=moved // part, transcendentals=0)


def ordered_rows(axis, features, order):
    rows = features.shape[0]
    place = lax.broadcasted_iota(jnp.int32, (rows, rows), 0) + lax.axis_index(axis) * rows
    chosen = (place == order[...]).astype(jnp.bfloat16)
    return lax.dot_general(
        chosen, features[...], (((0,), (0,)), ((), ())), preferred_element_type=jnp.float32
    )


def norm_kernel(axis, features, order, gain, normed, *parts):
    picked = ordered_rows(axis, features, order)
    factor = lax.rsqrt(jnp.mean(picked * picked, axis=-1, keepdims=True) + EPS)
    found = (picked * factor * gain[...]).astype(jnp.bfloat16)
    normed[...] = found
    size = found.shape[0] // len(parts)
    for index, part in enumerate(parts):
        part[...] = found[index * size : (index + 1) * size]


def prepare(features, order, gain):
    rows, width = features.shape
    half = jax.ShapeDtypeStruct((rows // 2, width), jnp.bfloat16)
    return pl.pallas_call(
        functools.partial(norm_kernel, "seq"),
        out_shape=[jax.ShapeDtypeStruct((rows, width), jnp.bfloat16), half, half],
        compiler_params=pltpu.CompilerParams(vmem_limit_bytes=16 * MIB),
        cost_estimate=cost(2 * rows * rows * width, 6 * rows * width),
        name="norm",
    )(features, order, gain.reshape(1, width))


def choose_kernel(axis, one, other, chosen, left, arrived):
    straight = lax.axis_index(axis) == 0

    def copies(first, second):
        return (
            pltpu.make_async_copy(first, chosen, arrived.at[0]),
            pltpu.make_async_copy(second, left, arrived.at[1]),
        )

    @pl.when(straight)
    def _():
        for copy in copies(one, other):
            copy.start()

    @pl.when(jnp.logical_not(straight))
    def _():
        for copy in copies(other, one):
            copy.start()

    for copy in copies(one, other):
        copy.wait()


def choose(axis, one, other):
    anywhere = pl.BlockSpec(memory_space=pl.ANY)
    local = pl.BlockSpec(memory_space=pltpu.VMEM)
    return pl.pallas_call(
        functools.partial(choose_kernel, axis),
        out_shape=[jax.ShapeDtypeStruct(one.shape, one.dtype)] * 2,
        in_specs=[anywhere, anywhere],
        out_specs=[local, local],
        scratch_shapes=[pltpu.SemaphoreType.DMA((2,))],
        compiler_params=pltpu.CompilerParams(vmem_limit_bytes=60 * MIB),
        cost_estimate=cost(0, 6 * one.size),
        name="choose",
    )(one, other)


def head_scale(values, head_dim, gain):
    columns = values.shape[1]
    row = lax.broadcasted_iota(jnp.int32, (columns, columns), 0) // head_dim
    column = lax.broadcasted_iota(jnp.int32, (columns, columns), 1) // head_dim
    same = (row == column).astype(jnp.bfloat16)
    sums = jnp.dot(
        (values * values).astype(jnp.bfloat16), same, preferred_element_type=jnp.float32
    )
    factor = lax.rsqrt(sums * (1.0 / head_dim) + EPS)
    return (values * factor * gain).astype(jnp.bfloat16)


def project_into(source, weights, first, head_dim, scaled, out):
    width = source.shape[1]
    chunk = 4 * head_dim
    at = 0
    for columns, gain in scaled:
        for _ in range(columns // chunk):
            found = jnp.dot(
                source, weights[:, first + at : first + at + chunk],
                preferred_element_type=jnp.float32,
            )
            out(at, found.astype(jnp.bfloat16) if gain is None else head_scale(found, head_dim, gain))
            at += chunk


def project_into(source, weights, first, head_dim, scaled, out):
    width = source.shape[1]
    chunk = 4 * head_dim
    at = 0
    for columns, gain in scaled:
        for _ in range(columns // chunk):
            found = jnp.dot(
                source, weights[:, first + at : first + at + chunk],
                preferred_element_type=jnp.float32,
            )
            out(at, found.astype(jnp.bfloat16) if gain is None else head_scale(found, head_dim, gain))
            at += chunk


def project_kernel(axis, head_dim, scale, count, with_queries, *refs):
    if with_queries:
        features, order, *refs, ordered, key_values, gathered = refs
        ordered[...] = ordered_rows(axis, features, order).astype(jnp.bfloat16)
        refs = [*refs, key_values, gathered]
    sources = refs[:count]
    weights, query_gain, key_gain, *rest = refs[count:]
    queries = rest[0] if with_queries else None
    key_values, gathered = rest[-2:]
    width = sources[0].shape[1]
    chunk = 4 * head_dim
    at = 0
    for source in sources:
        gathered[at : at + source.shape[0], :] = source[...]
        at += source.shape[0]

    def store_key_value(at, value):
        key_values[:, at : at + chunk] = value

    def store_query(at, value):
        queries[:, at : at + chunk] = value

    if with_queries:
        gain = query_gain[...] * scale
        project_into(sources[0][...], weights, 0, head_dim, [(width, gain)], store_query)
    project_into(
        gathered[...], weights, width, head_dim, [(width, key_gain[...]), (width, None)],
        store_key_value,
    )


def project(sources, weights, query_gain, key_gain, unordered=()):
    with_queries = bool(unordered)
    width = sources[0].shape[1]
    rows = sum(source.shape[0] for source in sources)
    head_dim = query_gain.shape[0]
    shapes = [jax.ShapeDtypeStruct((rows, 2 * width), jnp.bfloat16)]
    if with_queries:
        shapes = [jax.ShapeDtypeStruct(sources[0].shape, jnp.bfloat16)] * 2 + shapes
    local = pl.BlockSpec(memory_space=pltpu.VMEM)
    return pl.pallas_call(
        functools.partial(
            project_kernel, "seq", head_dim, 2.0 / math.sqrt(head_dim), len(sources), with_queries
        ),
        out_shape=shapes,
        in_specs=[local] * (len(unordered) + len(sources) + 3),
        out_specs=[local] * len(shapes),
        scratch_shapes=[pltpu.VMEM((rows, width), jnp.bfloat16)],
        compiler_params=pltpu.CompilerParams(vmem_limit_bytes=24 * MIB),
        cost_estimate=cost(4 * rows * width * width, 8 * width * width),
        name="project",
    )(*unordered, *sources, weights, jnp.tile(query_gain, 4)[None], jnp.tile(key_gain, 4)[None])


def slot_of(block, me, cycle, blocks):
    holder = lax.div(block, blocks)
    away = lax.rem(holder - me + REACH + cycle, cycle) - REACH
    turned = away * (1 - 2 * lax.rem(me, 2))
    return jnp.where(turned > 0, 2 * turned - 1, -2 * turned), lax.rem(block, blocks)


def pick_blocks(lists, counts, picks, at, me, cycle, blocks, wanted):
    found = 0
    count = counts[at]
    for index in range(MAXNZ):
        slot, place = slot_of(lists[at, index], me, cycle, blocks)
        take = (index < count) & wanted(slot)
        spot = found

        @pl.when(take)
        def _(slot=slot, place=place, spot=spot):
            picks[spot] = slot * blocks + place

        found = found + take.astype(jnp.int32)

    @pl.when(lax.rem(found, 2) == 1)
    def _(found=found):
        picks[found] = picks[found - 1]

    return found


def add_blocks(queries, window, picks, sums, here, count):
    width = queries.shape[1]
    pairs = sums.shape[0]
    pair = width // pairs
    low = lax.broadcasted_iota(jnp.int32, (BLOCK, pair), 1) < pair // 2
    key_lane = lax.broadcasted_iota(jnp.int32, (2 * BLOCK, 2 * BLOCK), 1)
    ones = jnp.ones((2 * BLOCK, pair), jnp.bfloat16)

    def two_blocks(step, carry):
        one = pl.ds(pl.multiple_of(picks[2 * step] * BLOCK, BLOCK), BLOCK)
        other = pl.ds(pl.multiple_of(picks[2 * step + 1] * BLOCK, BLOCK), BLOCK)
        kept = key_lane < jnp.where(2 * step + 1 < count, 2 * BLOCK, BLOCK)
        for index in range(pairs):
            columns = pl.ds(index * pair, pair)
            later = pl.ds(width + index * pair, pair)
            asked = queries[here, columns]
            none = jnp.zeros_like(asked)
            both = jnp.concatenate(
                [jnp.where(low, asked, none), jnp.where(low, none, asked)], axis=0
            )
            known = jnp.concatenate([window[one, columns], window[other, columns]], axis=0)
            held = jnp.concatenate([window[one, later], window[other, later]], axis=0)
            scores = lax.dot_general(
                both, known, (((1,), (1,)), ((), ())), preferred_element_type=jnp.float32
            )
            shares = jnp.where(kept, jnp.exp(scores), 0.0).astype(jnp.bfloat16)
            found = jnp.dot(
                shares, jnp.concatenate([held, ones], axis=1), preferred_element_type=jnp.float32
            )
            sums[index] = jnp.where(step == 0, found, sums[index] + found)
        return carry

    lax.fori_loop(0, lax.div(count + 1, 2), two_blocks, 0)


def attend_kernel(
    axis, cycle, lists, counts, queries, own_mate, near, across, mixed, totals,
    sums, window, picks,
):
    rows, width = queries.shape
    blocks = rows // BLOCK
    pairs = sums.shape[0]
    pair = width // pairs
    me = lax.axis_index(axis)
    low = lax.broadcasted_iota(jnp.int32, (BLOCK, pair), 1) < pair // 2
    window[: 2 * rows, :] = own_mate[...]
    window[2 * rows : 3 * rows, :] = near[...]
    window[3 * rows :, :] = across[...]
    for at in range(blocks):
        here = pl.ds(at * BLOCK, BLOCK)
        count = pick_blocks(
            lists, counts, picks, at, me, cycle, blocks, lambda slot: slot < 2 * REACH
        )
        add_blocks(queries, window, picks, sums, here, count)
        for index in range(pairs):
            total = sums[index]
            columns = pl.ds(index * pair, pair)
            mixed[here, columns] = jnp.where(low, total[:BLOCK, :pair], total[BLOCK:, :pair])
            totals[here, columns] = jnp.where(low, total[:BLOCK, pair:], total[BLOCK:, pair:])


def attend(axis, cycle, lists, counts, queries, sources):
    rows, width = queries.shape
    shape = jax.ShapeDtypeStruct((rows, width), jnp.float32)
    scalars = pl.BlockSpec(memory_space=pltpu.SMEM)
    local = pl.BlockSpec(memory_space=pltpu.VMEM)
    pairs = width // BLOCK
    slots = 2 * REACH
    work = 2 * rows * MAXNZ * BLOCK * width
    return pl.pallas_call(
        functools.partial(attend_kernel, axis, cycle),
        out_shape=(shape, shape),
        in_specs=[scalars, scalars, local] + [local] * len(sources),
        out_specs=(local, local),
        scratch_shapes=[
            pltpu.VMEM((pairs, 2 * BLOCK, 2 * BLOCK), jnp.float32),
            pltpu.VMEM((slots * rows, 2 * width), jnp.bfloat16),
            pltpu.SMEM((MAXNZ,), jnp.int32),
        ],
        compiler_params=pltpu.CompilerParams(vmem_limit_bytes=32 * MIB),
        cost_estimate=pl.CostEstimate(
            flops=ATTEND_COST, bytes_accessed=4 * slots * rows * width, transcendentals=0
        ),
        name="attend",
    )(lists, counts, queries, *sources)


def finish_kernel(
    axis, cycle, lists, counts, queries, window, mixed, totals, attention, sums, picks,
):
    rows, width = queries.shape
    blocks = rows // BLOCK
    pairs = sums.shape[0]
    pair = width // pairs
    me = lax.axis_index(axis)
    low = lax.broadcasted_iota(jnp.int32, (BLOCK, pair), 1) < pair // 2

    for at in range(blocks):
        here = pl.ds(at * BLOCK, BLOCK)
        count = pick_blocks(
            lists, counts, picks, at, me, cycle, blocks, lambda slot: slot == 2 * REACH
        )
        shift = 2 * REACH * blocks

        @pl.when(count == 0)
        def _():
            sums[...] = jnp.zeros_like(sums)

        for index in range(blocks + 1):
            picks[index] = jnp.clip(picks[index] - shift, 0, blocks - 1)
        add_blocks(queries, window, picks, sums, here, count)
        for index in range(pairs):
            total = sums[index]
            columns = pl.ds(index * pair, pair)
            share = (
                mixed[here, columns] + jnp.where(low, total[:BLOCK, :pair], total[BLOCK:, :pair])
            ) / (
                totals[here, columns] + jnp.where(low, total[:BLOCK, pair:], total[BLOCK:, pair:])
            )
            attention[here, columns] = share.astype(jnp.bfloat16)


def finish(
    axis, cycle, lists, counts, queries, far_kv, mixed, totals
):
    rows, width = queries.shape
    shape = jax.ShapeDtypeStruct((rows, width), jnp.bfloat16)
    scalars = pl.BlockSpec(memory_space=pltpu.SMEM)
    local = pl.BlockSpec(memory_space=pltpu.VMEM)
    pairs = width // BLOCK
    return pl.pallas_call(
        functools.partial(finish_kernel, axis, cycle),
        out_shape=shape,
        in_specs=[scalars, scalars] + [local] * 4,
        out_specs=local,
        scratch_shapes=[
            pltpu.VMEM((pairs, 2 * BLOCK, 2 * BLOCK), jnp.float32),
            pltpu.SMEM((MAXNZ,), jnp.int32),
        ],
        compiler_params=pltpu.CompilerParams(vmem_limit_bytes=32 * MIB),
        cost_estimate=cost(6 * rows * width * width, 8 * width * width),
        name="finish",
    )(
        lists, counts, queries, far_kv, mixed, totals
    )


def output_kernel(attention, ordered, weights, gain, attended, *seconds):
    product = jnp.dot(attention[...], weights[...], preferred_element_type=jnp.float32)
    result = (ordered[...].astype(jnp.float32) + product).astype(jnp.bfloat16)
    attended[...] = result
    widened = result.astype(jnp.float32)
    factor = lax.rsqrt(jnp.mean(widened * widened, axis=-1, keepdims=True) + EPS)
    second = (widened * factor * gain[...]).astype(jnp.bfloat16)
    part = second.shape[0] // len(seconds)
    for index, kept in enumerate(seconds):
        kept[...] = second[index * part : (index + 1) * part]


def attention_output(attention, ordered, weights, gain, parts):
    rows, width = attention.shape
    shape = jax.ShapeDtypeStruct((rows, width), jnp.bfloat16)
    return pl.pallas_call(
        output_kernel,
        out_shape=[shape] + [jax.ShapeDtypeStruct((rows // parts, width), jnp.bfloat16)] * parts,
        compiler_params=pltpu.CompilerParams(vmem_limit_bytes=24 * MIB),
        cost_estimate=cost(2 * rows * width * width, 2 * width * width),
        name="attention_output",
    )(attention, ordered, weights, gain.reshape(1, width))


def pieces_kernel(axis, swaps, sources, bases, has_known, *refs):
    count = len(swaps)
    seconds, refs = refs[:sources], refs[sources:]
    firsts, refs = refs[:count], refs[count:]
    lasts, refs = refs[:count], refs[count:]
    base, refs = refs[:bases], refs[bases:]
    known, results = (refs[0], refs[1:]) if has_known else (None, refs)
    straight = lax.axis_index(axis) == 0
    rows = jnp.concatenate([second[...] for second in seconds], axis=0)
    total = None
    for index, swapped in enumerate(swaps):
        first_rows, last_rows = firsts[index][...], lasts[index][...]
        if swapped:
            first_rows, last_rows = (
                jnp.where(straight, first_rows, last_rows),
                jnp.where(straight, last_rows, first_rows),
            )
        before = lax.dot_general(
            rows, first_rows, (((1,), (1,)), ((), ())), preferred_element_type=jnp.float32
        )
        active = jax.nn.gelu(before, approximate=True).astype(jnp.bfloat16)
        part = jnp.dot(active, last_rows, preferred_element_type=jnp.float32)
        total = part if total is None else total + part
    if bases:
        total = total + jnp.concatenate([part[...] for part in base], axis=0).astype(jnp.float32)
    if has_known:
        total = total + known[...]
    part = total.shape[0] // len(results)
    for index, result in enumerate(results):
        result[...] = total[index * part : (index + 1) * part].astype(result.dtype)


def feed_pieces(axis, seconds, pieces, base, dtype, parts=1, known=None):
    rows = sum(second.shape[0] for second in seconds)
    width = seconds[0].shape[1]
    hidden = sum(piece[0].shape[0] for piece in pieces)
    operands = [*seconds] + [piece[0] for piece in pieces] + [piece[1] for piece in pieces]
    return pl.pallas_call(
        functools.partial(
            pieces_kernel, axis, tuple(piece[2] for piece in pieces), len(seconds), len(base),
            known is not None,
        ),
        out_shape=[jax.ShapeDtypeStruct((rows // parts, width), dtype)] * parts,
        compiler_params=pltpu.CompilerParams(vmem_limit_bytes=24 * MIB),
        cost_estimate=cost(4 * rows * width * hidden, 4 * hidden * width),
        name="feed_pieces",
    )(*operands, *base, *([] if known is None else [known]))


def total_kernel(attended, own, *refs):
    *returned, result = refs
    part = result.shape[0] // len(returned)
    for index, back in enumerate(returned):
        here = pl.ds(index * part, part)
        result[here, :] = (
            attended[here, :].astype(jnp.float32) + own[here, :] + back[...].astype(jnp.float32)
        ).astype(result.dtype)


def total_of(attended, own, returned):
    return pl.pallas_call(
        total_kernel,
        out_shape=jax.ShapeDtypeStruct(attended.shape, attended.dtype),
        compiler_params=pltpu.CompilerParams(vmem_limit_bytes=16 * MIB),
        cost_estimate=cost(attended.size, 10 * attended.size),
        name="total",
    )(attended, own, *returned)


def feed_kernel(steps, second, first_rows, second_rows, attended, result, total):
    step = pl.program_id(0)
    before = lax.dot_general(
        second[...], first_rows[...], (((1,), (1,)), ((), ())), preferred_element_type=jnp.float32
    )
    active = jax.nn.gelu(before, approximate=True).astype(jnp.bfloat16)
    part = jnp.dot(active, second_rows[...], preferred_element_type=jnp.float32)

    @pl.when(step == 0)
    def _():
        total[...] = part

    @pl.when(step > 0)
    def _():
        total[...] += part

    @pl.when(step == steps - 1)
    def _():
        result[...] = (attended[...].astype(jnp.float32) + total[...]).astype(jnp.bfloat16)


def feed_forward(second, first_rows, second_rows, attended):
    rows, width = second.shape
    hidden = first_rows.shape[0]
    chunk = min(512, hidden)
    steps = hidden // chunk
    whole = pl.BlockSpec((rows, width), lambda i: (0, 0))
    part = pl.BlockSpec((chunk, width), lambda i: (i, 0))
    return pl.pallas_call(
        functools.partial(feed_kernel, steps),
        out_shape=jax.ShapeDtypeStruct((rows, width), jnp.bfloat16),
        grid=(steps,),
        in_specs=[whole, part, part, whole],
        out_specs=whole,
        scratch_shapes=[pltpu.VMEM((rows, width), jnp.float32)],
        compiler_params=pltpu.CompilerParams(vmem_limit_bytes=40 * MIB),
        cost_estimate=pl.CostEstimate(
            flops=4 * rows * width * hidden,
            bytes_accessed=4 * hidden * width + 6 * rows * width,
            transcendentals=rows * hidden,
        ),
        name="feed_forward",
    )(second, first_rows, second_rows, attended)


def shards(
    pore_features,
    pore_order,
    block_lists,
    block_counts,
    norm1_gain,
    w_qkv,
    query_gain,
    key_gain,
    w_attn_out,
    norm2_gain,
    w_in,
    w_out,
):
    rows = pore_features.shape[0]
    cycle = lax.axis_size("seq")
    me = lax.axis_index("seq")

    def moved(value, where):
        return lax.ppermute(value, "seq", [(i, where(i) % cycle) for i in range(cycle)])

    def mate_of(value):
        return moved(value, lambda i: i + 1 - 2 * (i % 2))

    chip_rows, chip_columns = chip_grid(cycle // 2)
    lane = 2 * chip_columns

    def along(value, targets):
        pairs = [(lane * a + k, lane * b + k) for a, b in targets for k in range(lane)]
        return lax.ppermute(value, "seq", pairs)

    def beside(value):
        return moved(value, lambda i: i + 2 - 4 * (i // 2 % 2))

    def over(value):
        return lax.ppermute(value, "parts", [(0, 1), (1, 0)])

    shared = (chip_rows, chip_columns) == (4, 2) and lax.axis_size("parts") == 2
    if shared:
        swap = [(0, 1), (1, 0), (2, 3), (3, 2)]
        prime, left = choose("parts", w_in, w_out)
        pair_rows = along(prime, swap)
        third = along(prime, [(0, 2), (1, 3), (2, 0), (3, 1)])
    order = pore_order.reshape(1, rows)
    normed, *normed_parts = prepare(pore_features, order, norm1_gain)
    near = [moved(part, lambda i: i - 1 + 2 * (i % 2)) for part in normed_parts]
    mate = mate_of(normed)
    queries, ordered, own_mate = project(
        [normed, mate], w_qkv, query_gain, key_gain, (pore_features, order)
    )
    queries, late_normed, *near = lax.optimization_barrier((queries, normed, *near))
    far = moved(late_normed, lambda i: i + 2 - 4 * (i % 2))
    across = [mate_of(piece) for part in near for piece in jnp.split(part, 2)]

    (near_kv,) = project(near, w_qkv, query_gain, key_gain)
    if shared:
        near_kv, *across = lax.optimization_barrier((near_kv, *across))
    (across_kv,) = project(across, w_qkv, query_gain, key_gain)
    mixed, totals = attend(
        "seq", cycle, block_lists, block_counts, queries, [own_mate, near_kv, across_kv]
    )
    if shared:
        mixed, totals, third, pair_rows, left = lax.optimization_barrier(
            (mixed, totals, third, pair_rows, left)
        )
        other_pair = along(left, swap)
        fourth = along(third, swap)
        other_third = over(third)
        mixed, totals, far = lax.optimization_barrier((mixed, totals, far))
    (far_kv,) = project([far], w_qkv, query_gain, key_gain)
    attention = finish(
        "seq", cycle, block_lists, block_counts, queries, far_kv, mixed, totals
    )
    parts = 2 if shared else 1
    attended, *seconds = attention_output(attention, ordered, w_attn_out, norm2_gain, parts)
    if shared:
        guests = [beside(second) for second in seconds]
        mate_seconds = [mate_of(second) for second in seconds]
        attended, fourth = lax.optimization_barrier((attended, fourth))
        guests[0], other_pair, other_third = lax.optimization_barrier(
            (guests[0], other_pair, other_third)
        )
        other_fourth = over(fourth)
        pieces = [
            (w_in, w_out, False),
            (pair_rows, other_pair, True),
            (third, other_third, True),
        ]
        guest_mate_parts = feed_pieces(
            "parts", [mate_of(guest) for guest in guests], pieces, [], jnp.bfloat16, parts
        )
        other_fourth, *guest_mate_parts = lax.optimization_barrier(
            (other_fourth, *guest_mate_parts)
        )
        last = [
            (fourth, other_fourth, True),
            (mate_of(fourth), mate_of(other_fourth), True),
        ]
        guest_parts = feed_pieces("parts", guests, pieces, [], jnp.float32, parts)
        returned = []
        for guest, part, base in zip(guests, guest_parts, guest_mate_parts):
            (guest_part,) = feed_pieces(
                "parts", [guest], last, [mate_of(base)], jnp.bfloat16, 1, part
            )
            returned.append(beside(guest_part))
        mate_parts = feed_pieces("parts", mate_seconds, pieces, [], jnp.bfloat16, 4)
        (own_main,) = feed_pieces("parts", seconds, pieces, [], jnp.float32)
        returned[0], own_main = lax.optimization_barrier((returned[0], own_main))
        (own_part,) = feed_pieces(
            "parts", seconds, last, [mate_of(part) for part in mate_parts], jnp.float32, 1, own_main
        )
        layer_output = total_of(attended, own_part, returned)
    else:
        ring = [2 * chip + core for chip in chip_cycle(cycle // 2) for core in range(2)]
        gathered_in = lax.all_gather(w_in, "seq", axis=0, tiled=True, axis_index_groups=[ring])
        gathered_out = lax.all_gather(w_out, "seq", axis=0, tiled=True, axis_index_groups=[ring])
        layer_output = feed_forward(seconds[0], gathered_in, gathered_out, attended)
    return (attended, layer_output)


def solution(mesh):
    return jax.shard_map(
        shards,
        mesh=mesh,
        in_specs=(
            P(("parts", "seq"), None),
            P(("parts", "seq")),
            P(("parts", "seq"), None),
            P(("parts", "seq")),
            P(),
            P(),
            P(),
            P(),
            P(),
            P(),
            P("seq", None),
            P("seq", None),
        ),
        out_specs=(P(("parts", "seq"), None), P(("parts", "seq"), None)),
        check_vma=False,
    )
```

```python
import functools
import math

import jax
import jax.numpy as jnp
from jax import lax
from jax.experimental import pallas as pl
from jax.experimental.pallas import tpu as pltpu
from jax.sharding import PartitionSpec as P

HEADS = 16
BLOCK = 128
REACH = 2
MAXNZ = 8
EPS = 1e-06
ATTEND_COST = 5 * 10**8
MIB = 1024 * 1024


def chip_grid(chips):
    columns = 1 << ((chips.bit_length() - 1) // 2)
    return chips // columns, columns


def chip_cycle(chips):
    rows, columns = chip_grid(chips)
    if columns < 2 or rows % 2:
        return list(range(chips))
    order = [(row, 0) for row in range(rows)]
    for row in reversed(range(rows)):
        inner = list(range(1, columns))
        order += [(row, column) for column in (inner if (rows - 1 - row) % 2 == 0 else inner[::-1])]
    return [row * columns + column for row, column in order]


def cost(flops, moved, part=64):
    return pl.CostEstimate(flops=flops // part, bytes_accessed=moved // part, transcendentals=0)


def ordered_rows(axis, features, order):
    rows = features.shape[0]
    place = lax.broadcasted_iota(jnp.int32, (rows, rows), 0) + lax.axis_index(axis) * rows
    chosen = (place == order[...]).astype(jnp.bfloat16)
    return lax.dot_general(
        chosen, features[...], (((0,), (0,)), ((), ())), preferred_element_type=jnp.float32
    )


def norm_kernel(axis, features, order, gain, normed, *parts):
    picked = ordered_rows(axis, features, order)
    factor = lax.rsqrt(jnp.mean(picked * picked, axis=-1, keepdims=True) + EPS)
    found = (picked * factor * gain[...]).astype(jnp.bfloat16)
    normed[...] = found
    size = found.shape[0] // len(parts)
    for index, part in enumerate(parts):
        part[...] = found[index * size : (index + 1) * size]


def prepare(features, order, gain):
    rows, width = features.shape
    half = jax.ShapeDtypeStruct((rows // 2, width), jnp.bfloat16)
    return pl.pallas_call(
        functools.partial(norm_kernel, "seq"),
        out_shape=[jax.ShapeDtypeStruct((rows, width), jnp.bfloat16), half, half],
        compiler_params=pltpu.CompilerParams(vmem_limit_bytes=16 * MIB),
        cost_estimate=cost(2 * rows * rows * width, 6 * rows * width),
        name="norm",
    )(features, order, gain.reshape(1, width))


def choose_kernel(axis, one, other, chosen, left, arrived):
    straight = lax.axis_index(axis) == 0

    def copies(first, second):
        return (
            pltpu.make_async_copy(first, chosen, arrived.at[0]),
            pltpu.make_async_copy(second, left, arrived.at[1]),
        )

    @pl.when(straight)
    def _():
        for copy in copies(one, other):
            copy.start()

    @pl.when(jnp.logical_not(straight))
    def _():
        for copy in copies(other, one):
            copy.start()

    for copy in copies(one, other):
        copy.wait()


def choose(axis, one, other):
    anywhere = pl.BlockSpec(memory_space=pl.ANY)
    local = pl.BlockSpec(memory_space=pltpu.VMEM)
    return pl.pallas_call(
        functools.partial(choose_kernel, axis),
        out_shape=[jax.ShapeDtypeStruct(one.shape, one.dtype)] * 2,
        in_specs=[anywhere, anywhere],
        out_specs=[local, local],
        scratch_shapes=[pltpu.SemaphoreType.DMA((2,))],
        compiler_params=pltpu.CompilerParams(vmem_limit_bytes=60 * MIB),
        cost_estimate=cost(0, 6 * one.size),
        name="choose",
    )(one, other)


def head_scale(values, head_dim, gain):
    columns = values.shape[1]
    row = lax.broadcasted_iota(jnp.int32, (columns, columns), 0) // head_dim
    column = lax.broadcasted_iota(jnp.int32, (columns, columns), 1) // head_dim
    same = (row == column).astype(jnp.bfloat16)
    sums = jnp.dot(
        (values * values).astype(jnp.bfloat16), same, preferred_element_type=jnp.float32
    )
    factor = lax.rsqrt(sums * (1.0 / head_dim) + EPS)
    return (values * factor * gain).astype(jnp.bfloat16)


def project_into(source, weights, first, head_dim, scaled, out):
    width = source.shape[1]
    chunk = 4 * head_dim
    at = 0
    for columns, gain in scaled:
        for _ in range(columns // chunk):
            found = jnp.dot(
                source, weights[:, first + at : first + at + chunk],
                preferred_element_type=jnp.float32,
            )
            out(at, found.astype(jnp.bfloat16) if gain is None else head_scale(found, head_dim, gain))
            at += chunk


def project_into(source, weights, first, head_dim, scaled, out):
    width = source.shape[1]
    chunk = 4 * head_dim
    at = 0
    for columns, gain in scaled:
        for _ in range(columns // chunk):
            found = jnp.dot(
                source, weights[:, first + at : first + at + chunk],
                preferred_element_type=jnp.float32,
            )
            out(at, found.astype(jnp.bfloat16) if gain is None else head_scale(found, head_dim, gain))
            at += chunk


def project_kernel(axis, head_dim, scale, count, with_queries, *refs):
    if with_queries:
        features, order, *refs, ordered, key_values, gathered = refs
        ordered[...] = ordered_rows(axis, features, order).astype(jnp.bfloat16)
        refs = [*refs, key_values, gathered]
    sources = refs[:count]
    weights, query_gain, key_gain, *rest = refs[count:]
    queries = rest[0] if with_queries else None
    key_values, gathered = rest[-2:]
    width = sources[0].shape[1]
    chunk = 4 * head_dim
    at = 0
    for source in sources:
        gathered[at : at + source.shape[0], :] = source[...]
        at += source.shape[0]

    def store_key_value(at, value):
        key_values[:, at : at + chunk] = value

    def store_query(at, value):
        queries[:, at : at + chunk] = value

    if with_queries:
        gain = query_gain[...] * scale
        project_into(sources[0][...], weights, 0, head_dim, [(width, gain)], store_query)
    project_into(
        gathered[...], weights, width, head_dim, [(width, key_gain[...]), (width, None)],
        store_key_value,
    )


def project(sources, weights, query_gain, key_gain, unordered=()):
    with_queries = bool(unordered)
    width = sources[0].shape[1]
    rows = sum(source.shape[0] for source in sources)
    head_dim = query_gain.shape[0]
    shapes = [jax.ShapeDtypeStruct((rows, 2 * width), jnp.bfloat16)]
    if with_queries:
        shapes = [jax.ShapeDtypeStruct(sources[0].shape, jnp.bfloat16)] * 2 + shapes
    local = pl.BlockSpec(memory_space=pltpu.VMEM)
    return pl.pallas_call(
        functools.partial(
            project_kernel, "seq", head_dim, 2.0 / math.sqrt(head_dim), len(sources), with_queries
        ),
        out_shape=shapes,
        in_specs=[local] * (len(unordered) + len(sources) + 3),
        out_specs=[local] * len(shapes),
        scratch_shapes=[pltpu.VMEM((rows, width), jnp.bfloat16)],
        compiler_params=pltpu.CompilerParams(vmem_limit_bytes=24 * MIB),
        cost_estimate=cost(4 * rows * width * width, 8 * width * width),
        name="project",
    )(*unordered, *sources, weights, jnp.tile(query_gain, 4)[None], jnp.tile(key_gain, 4)[None])


def slot_of(block, me, cycle, blocks):
    holder = lax.div(block, blocks)
    away = lax.rem(holder - me + REACH + cycle, cycle) - REACH
    turned = away * (1 - 2 * lax.rem(me, 2))
    return jnp.where(turned > 0, 2 * turned - 1, -2 * turned), lax.rem(block, blocks)


def pick_blocks(lists, counts, picks, at, me, cycle, blocks, wanted):
    found = 0
    count = counts[at]
    for index in range(MAXNZ):
        slot, place = slot_of(lists[at, index], me, cycle, blocks)
        take = (index < count) & wanted(slot)
        spot = found

        @pl.when(take)
        def _(slot=slot, place=place, spot=spot):
            picks[spot] = slot * blocks + place

        found = found + take.astype(jnp.int32)

    @pl.when(lax.rem(found, 2) == 1)
    def _(found=found):
        picks[found] = picks[found - 1]

    return found


def add_blocks(queries, window, picks, sums, here, count):
    width = queries.shape[1]
    pairs = sums.shape[0]
    pair = width // pairs
    low = lax.broadcasted_iota(jnp.int32, (BLOCK, pair), 1) < pair // 2
    key_lane = lax.broadcasted_iota(jnp.int32, (2 * BLOCK, 2 * BLOCK), 1)
    ones = jnp.ones((2 * BLOCK, pair), jnp.bfloat16)

    def two_blocks(step, carry):
        one = pl.ds(pl.multiple_of(picks[2 * step] * BLOCK, BLOCK), BLOCK)
        other = pl.ds(pl.multiple_of(picks[2 * step + 1] * BLOCK, BLOCK), BLOCK)
        kept = key_lane < jnp.where(2 * step + 1 < count, 2 * BLOCK, BLOCK)
        for index in range(pairs):
            columns = pl.ds(index * pair, pair)
            later = pl.ds(width + index * pair, pair)
            asked = queries[here, columns]
            none = jnp.zeros_like(asked)
            both = jnp.concatenate(
                [jnp.where(low, asked, none), jnp.where(low, none, asked)], axis=0
            )
            known = jnp.concatenate([window[one, columns], window[other, columns]], axis=0)
            held = jnp.concatenate([window[one, later], window[other, later]], axis=0)
            scores = lax.dot_general(
                both, known, (((1,), (1,)), ((), ())), preferred_element_type=jnp.float32
            )
            shares = jnp.where(kept, jnp.exp(scores), 0.0).astype(jnp.bfloat16)
            found = jnp.dot(
                shares, jnp.concatenate([held, ones], axis=1), preferred_element_type=jnp.float32
            )
            sums[index] = jnp.where(step == 0, found, sums[index] + found)
        return carry

    lax.fori_loop(0, lax.div(count + 1, 2), two_blocks, 0)


def attend_kernel(
    axis, cycle, lists, counts, queries, own_mate, near, across, mixed, totals,
    sums, window, picks,
):
    rows, width = queries.shape
    blocks = rows // BLOCK
    pairs = sums.shape[0]
    pair = width // pairs
    me = lax.axis_index(axis)
    low = lax.broadcasted_iota(jnp.int32, (BLOCK, pair), 1) < pair // 2
    window[: 2 * rows, :] = own_mate[...]
    window[2 * rows : 3 * rows, :] = near[...]
    window[3 * rows :, :] = across[...]
    for at in range(blocks):
        here = pl.ds(at * BLOCK, BLOCK)
        count = pick_blocks(
            lists, counts, picks, at, me, cycle, blocks, lambda slot: slot < 2 * REACH
        )
        add_blocks(queries, window, picks, sums, here, count)
        for index in range(pairs):
            total = sums[index]
            columns = pl.ds(index * pair, pair)
            mixed[here, columns] = jnp.where(low, total[:BLOCK, :pair], total[BLOCK:, :pair])
            totals[here, columns] = jnp.where(low, total[:BLOCK, pair:], total[BLOCK:, pair:])


def attend(axis, cycle, lists, counts, queries, sources):
    rows, width = queries.shape
    shape = jax.ShapeDtypeStruct((rows, width), jnp.float32)
    scalars = pl.BlockSpec(memory_space=pltpu.SMEM)
    local = pl.BlockSpec(memory_space=pltpu.VMEM)
    pairs = width // BLOCK
    slots = 2 * REACH
    work = 2 * rows * MAXNZ * BLOCK * width
    return pl.pallas_call(
        functools.partial(attend_kernel, axis, cycle),
        out_shape=(shape, shape),
        in_specs=[scalars, scalars, local] + [local] * len(sources),
        out_specs=(local, local),
        scratch_shapes=[
            pltpu.VMEM((pairs, 2 * BLOCK, 2 * BLOCK), jnp.float32),
            pltpu.VMEM((slots * rows, 2 * width), jnp.bfloat16),
            pltpu.SMEM((MAXNZ,), jnp.int32),
        ],
        compiler_params=pltpu.CompilerParams(vmem_limit_bytes=32 * MIB),
        cost_estimate=pl.CostEstimate(
            flops=ATTEND_COST, bytes_accessed=4 * slots * rows * width, transcendentals=0
        ),
        name="attend",
    )(lists, counts, queries, *sources)


def finish_kernel(
    axis, cycle, lists, counts, queries, window, mixed, totals, attention, sums, picks,
):
    rows, width = queries.shape
    blocks = rows // BLOCK
    pairs = sums.shape[0]
    pair = width // pairs
    me = lax.axis_index(axis)
    low = lax.broadcasted_iota(jnp.int32, (BLOCK, pair), 1) < pair // 2

    for at in range(blocks):
        here = pl.ds(at * BLOCK, BLOCK)
        count = pick_blocks(
            lists, counts, picks, at, me, cycle, blocks, lambda slot: slot == 2 * REACH
        )
        shift = 2 * REACH * blocks

        @pl.when(count == 0)
        def _():
            sums[...] = jnp.zeros_like(sums)

        for index in range(blocks + 1):
            picks[index] = jnp.clip(picks[index] - shift, 0, blocks - 1)
        add_blocks(queries, window, picks, sums, here, count)
        for index in range(pairs):
            total = sums[index]
            columns = pl.ds(index * pair, pair)
            share = (
                mixed[here, columns] + jnp.where(low, total[:BLOCK, :pair], total[BLOCK:, :pair])
            ) / (
                totals[here, columns] + jnp.where(low, total[:BLOCK, pair:], total[BLOCK:, pair:])
            )
            attention[here, columns] = share.astype(jnp.bfloat16)


def finish(
    axis, cycle, lists, counts, queries, far_kv, mixed, totals
):
    rows, width = queries.shape
    shape = jax.ShapeDtypeStruct((rows, width), jnp.bfloat16)
    scalars = pl.BlockSpec(memory_space=pltpu.SMEM)
    local = pl.BlockSpec(memory_space=pltpu.VMEM)
    pairs = width // BLOCK
    return pl.pallas_call(
        functools.partial(finish_kernel, axis, cycle),
        out_shape=shape,
        in_specs=[scalars, scalars] + [local] * 4,
        out_specs=local,
        scratch_shapes=[
            pltpu.VMEM((pairs, 2 * BLOCK, 2 * BLOCK), jnp.float32),
            pltpu.SMEM((MAXNZ,), jnp.int32),
        ],
        compiler_params=pltpu.CompilerParams(vmem_limit_bytes=32 * MIB),
        cost_estimate=cost(6 * rows * width * width, 8 * width * width),
        name="finish",
    )(
        lists, counts, queries, far_kv, mixed, totals
    )


def output_kernel(attention, ordered, weights, gain, attended, *seconds):
    product = jnp.dot(attention[...], weights[...], preferred_element_type=jnp.float32)
    result = (ordered[...].astype(jnp.float32) + product).astype(jnp.bfloat16)
    attended[...] = result
    widened = result.astype(jnp.float32)
    factor = lax.rsqrt(jnp.mean(widened * widened, axis=-1, keepdims=True) + EPS)
    second = (widened * factor * gain[...]).astype(jnp.bfloat16)
    part = second.shape[0] // len(seconds)
    for index, kept in enumerate(seconds):
        kept[...] = second[index * part : (index + 1) * part]


def attention_output(attention, ordered, weights, gain, parts):
    rows, width = attention.shape
    shape = jax.ShapeDtypeStruct((rows, width), jnp.bfloat16)
    return pl.pallas_call(
        output_kernel,
        out_shape=[shape] + [jax.ShapeDtypeStruct((rows // parts, width), jnp.bfloat16)] * parts,
        compiler_params=pltpu.CompilerParams(vmem_limit_bytes=24 * MIB),
        cost_estimate=cost(2 * rows * width * width, 2 * width * width),
        name="attention_output",
    )(attention, ordered, weights, gain.reshape(1, width))


def pieces_kernel(axis, swaps, sources, bases, has_known, *refs):
    count = len(swaps)
    seconds, refs = refs[:sources], refs[sources:]
    firsts, refs = refs[:count], refs[count:]
    lasts, refs = refs[:count], refs[count:]
    base, refs = refs[:bases], refs[bases:]
    known, results = (refs[0], refs[1:]) if has_known else (None, refs)
    straight = lax.axis_index(axis) == 0
    rows = jnp.concatenate([second[...] for second in seconds], axis=0)
    total = None
    for index, swapped in enumerate(swaps):
        first_rows, last_rows = firsts[index][...], lasts[index][...]
        if swapped:
            first_rows, last_rows = (
                jnp.where(straight, first_rows, last_rows),
                jnp.where(straight, last_rows, first_rows),
            )
        before = lax.dot_general(
            rows, first_rows, (((1,), (1,)), ((), ())), preferred_element_type=jnp.float32
        )
        active = jax.nn.gelu(before, approximate=True).astype(jnp.bfloat16)
        part = jnp.dot(active, last_rows, preferred_element_type=jnp.float32)
        total = part if total is None else total + part
    if bases:
        total = total + jnp.concatenate([part[...] for part in base], axis=0).astype(jnp.float32)
    if has_known:
        total = total + known[...]
    part = total.shape[0] // len(results)
    for index, result in enumerate(results):
        result[...] = total[index * part : (index + 1) * part].astype(result.dtype)


def feed_pieces(axis, seconds, pieces, base, dtype, parts=1, known=None):
    rows = sum(second.shape[0] for second in seconds)
    width = seconds[0].shape[1]
    hidden = sum(piece[0].shape[0] for piece in pieces)
    operands = [*seconds] + [piece[0] for piece in pieces] + [piece[1] for piece in pieces]
    return pl.pallas_call(
        functools.partial(
            pieces_kernel, axis, tuple(piece[2] for piece in pieces), len(seconds), len(base),
            known is not None,
        ),
        out_shape=[jax.ShapeDtypeStruct((rows // parts, width), dtype)] * parts,
        compiler_params=pltpu.CompilerParams(vmem_limit_bytes=24 * MIB),
        cost_estimate=cost(4 * rows * width * hidden, 4 * hidden * width),
        name="feed_pieces",
    )(*operands, *base, *([] if known is None else [known]))


def total_kernel(attended, own, *refs):
    *returned, result = refs
    part = result.shape[0] // len(returned)
    for index, back in enumerate(returned):
        here = pl.ds(index * part, part)
        result[here, :] = (
            attended[here, :].astype(jnp.float32) + own[here, :] + back[...].astype(jnp.float32)
        ).astype(result.dtype)


def total_of(attended, own, returned):
    return pl.pallas_call(
        total_kernel,
        out_shape=jax.ShapeDtypeStruct(attended.shape, attended.dtype),
        compiler_params=pltpu.CompilerParams(vmem_limit_bytes=16 * MIB),
        cost_estimate=cost(attended.size, 10 * attended.size),
        name="total",
    )(attended, own, *returned)


def feed_kernel(steps, second, first_rows, second_rows, attended, result, total):
    step = pl.program_id(0)
    before = lax.dot_general(
        second[...], first_rows[...], (((1,), (1,)), ((), ())), preferred_element_type=jnp.float32
    )
    active = jax.nn.gelu(before, approximate=True).astype(jnp.bfloat16)
    part = jnp.dot(active, second_rows[...], preferred_element_type=jnp.float32)

    @pl.when(step == 0)
    def _():
        total[...] = part

    @pl.when(step > 0)
    def _():
        total[...] += part

    @pl.when(step == steps - 1)
    def _():
        result[...] = (attended[...].astype(jnp.float32) + total[...]).astype(jnp.bfloat16)


def feed_forward(second, first_rows, second_rows, attended):
    rows, width = second.shape
    hidden = first_rows.shape[0]
    chunk = min(512, hidden)
    steps = hidden // chunk
    whole = pl.BlockSpec((rows, width), lambda i: (0, 0))
    part = pl.BlockSpec((chunk, width), lambda i: (i, 0))
    return pl.pallas_call(
        functools.partial(feed_kernel, steps),
        out_shape=jax.ShapeDtypeStruct((rows, width), jnp.bfloat16),
        grid=(steps,),
        in_specs=[whole, part, part, whole],
        out_specs=whole,
        scratch_shapes=[pltpu.VMEM((rows, width), jnp.float32)],
        compiler_params=pltpu.CompilerParams(vmem_limit_bytes=40 * MIB),
        cost_estimate=pl.CostEstimate(
            flops=4 * rows * width * hidden,
            bytes_accessed=4 * hidden * width + 6 * rows * width,
            transcendentals=rows * hidden,
        ),
        name="feed_forward",
    )(second, first_rows, second_rows, attended)


def shards(
    pore_features,
    pore_order,
    block_lists,
    block_counts,
    norm1_gain,
    w_qkv,
    query_gain,
    key_gain,
    w_attn_out,
    norm2_gain,
    w_in,
    w_out,
):
    rows = pore_features.shape[0]
    cycle = lax.axis_size("seq")
    me = lax.axis_index("seq")

    def moved(value, where):
        return lax.ppermute(value, "seq", [(i, where(i) % cycle) for i in range(cycle)])

    def mate_of(value):
        return moved(value, lambda i: i + 1 - 2 * (i % 2))

    chip_rows, chip_columns = chip_grid(cycle // 2)
    lane = 2 * chip_columns

    def along(value, targets):
        pairs = [(lane * a + k, lane * b + k) for a, b in targets for k in range(lane)]
        return lax.ppermute(value, "seq", pairs)

    def beside(value):
        return moved(value, lambda i: i + 2 - 4 * (i // 2 % 2))

    def over(value):
        return lax.ppermute(value, "parts", [(0, 1), (1, 0)])

    shared = (chip_rows, chip_columns) == (4, 2) and lax.axis_size("parts") == 2
    if shared:
        swap = [(0, 1), (1, 0), (2, 3), (3, 2)]
        prime, left = choose("parts", w_in, w_out)
        pair_rows = along(prime, swap)
        third = along(prime, [(0, 2), (1, 3), (2, 0), (3, 1)])
    order = pore_order.reshape(1, rows)
    normed, *normed_parts = prepare(pore_features, order, norm1_gain)
    near = [moved(part, lambda i: i - 1 + 2 * (i % 2)) for part in normed_parts]
    mate = mate_of(normed)
    queries, ordered, own_mate = project(
        [normed, mate], w_qkv, query_gain, key_gain, (pore_features, order)
    )
    queries, late_normed, *near = lax.optimization_barrier((queries, normed, *near))
    far = moved(late_normed, lambda i: i + 2 - 4 * (i % 2))
    across = [mate_of(piece) for part in near for piece in jnp.split(part, 2)]

    (near_kv,) = project(near, w_qkv, query_gain, key_gain)
    if shared:
        near_kv, *across = lax.optimization_barrier((near_kv, *across))
    (across_kv,) = project(across, w_qkv, query_gain, key_gain)
    mixed, totals = attend(
        "seq", cycle, block_lists, block_counts, queries, [own_mate, near_kv, across_kv]
    )
    if shared:
        mixed, totals, third, pair_rows, left = lax.optimization_barrier(
            (mixed, totals, third, pair_rows, left)
        )
        other_pair = along(left, swap)
        fourth = along(third, swap)
        other_third = over(third)
        mixed, totals, far = lax.optimization_barrier((mixed, totals, far))
    (far_kv,) = project([far], w_qkv, query_gain, key_gain)
    attention = finish(
        "seq", cycle, block_lists, block_counts, queries, far_kv, mixed, totals
    )
    parts = 2 if shared else 1
    attended, *seconds = attention_output(attention, ordered, w_attn_out, norm2_gain, parts)
    if shared:
        guests = [beside(second) for second in seconds]
        mate_seconds = [mate_of(second) for second in seconds]
        attended, fourth = lax.optimization_barrier((attended, fourth))
        guests[0], other_pair, other_third = lax.optimization_barrier(
            (guests[0], other_pair, other_third)
        )
        other_fourth = over(fourth)
        pieces = [
            (w_in, w_out, False),
            (pair_rows, other_pair, True),
            (third, other_third, True),
        ]
        guest_mate_parts = []
        guest_parts = []
        for index in range(parts):
            guest_mate_parts += feed_pieces(
                "parts", [mate_of(part) for part in jnp.split(guests[index], 2)], pieces, [], jnp.bfloat16
            )
            guest_parts += feed_pieces("parts", [guests[index]], pieces, [], jnp.float32)
            if index == 0:
                guests[1], guest_mate_parts[0], guest_parts[0], other_fourth = (
                    lax.optimization_barrier(
                        (guests[1], guest_mate_parts[0], guest_parts[0], other_fourth)
                    )
                )
        last = [
            (fourth, other_fourth, True),
            (mate_of(fourth), mate_of(other_fourth), True),
        ]
        returned = []
        for guest, part, base in zip(guests, guest_parts, guest_mate_parts):
            (guest_part,) = feed_pieces(
                "parts", [guest], last, [mate_of(base)], jnp.bfloat16, 1, part
            )
            returned.append(beside(guest_part))
        mate_parts = feed_pieces("parts", mate_seconds, pieces, [], jnp.bfloat16, 4)
        (own_main,) = feed_pieces("parts", seconds, pieces, [], jnp.float32)
        returned[0], own_main = lax.optimization_barrier((returned[0], own_main))
        (own_part,) = feed_pieces(
            "parts", seconds, last, [mate_of(part) for part in mate_parts], jnp.float32, 1, own_main
        )
        layer_output = total_of(attended, own_part, returned)
    else:
        ring = [2 * chip + core for chip in chip_cycle(cycle // 2) for core in range(2)]
        gathered_in = lax.all_gather(w_in, "seq", axis=0, tiled=True, axis_index_groups=[ring])
        gathered_out = lax.all_gather(w_out, "seq", axis=0, tiled=True, axis_index_groups=[ring])
        layer_output = feed_forward(seconds[0], gathered_in, gathered_out, attended)
    return (attended, layer_output)


def solution(mesh):
    return jax.shard_map(
        shards,
        mesh=mesh,
        in_specs=(
            P(("parts", "seq"), None),
            P(("parts", "seq")),
            P(("parts", "seq"), None),
            P(("parts", "seq")),
            P(),
            P(),
            P(),
            P(),
            P(),
            P(),
            P("seq", None),
            P("seq", None),
        ),
        out_specs=(P(("parts", "seq"), None), P(("parts", "seq"), None)),
        check_vma=False,
    )
```

```python
import functools
import math

import jax
import jax.numpy as jnp
from jax import lax
from jax.experimental import pallas as pl
from jax.experimental.pallas import tpu as pltpu
from jax.sharding import PartitionSpec as P

HEADS = 16
BLOCK = 128
REACH = 2
MAXNZ = 8
EPS = 1e-06
ATTEND_COST = 5 * 10**8
MIB = 1024 * 1024


def chip_grid(chips):
    columns = 1 << ((chips.bit_length() - 1) // 2)
    return chips // columns, columns


def chip_cycle(chips):
    rows, columns = chip_grid(chips)
    if columns < 2 or rows % 2:
        return list(range(chips))
    order = [(row, 0) for row in range(rows)]
    for row in reversed(range(rows)):
        inner = list(range(1, columns))
        order += [(row, column) for column in (inner if (rows - 1 - row) % 2 == 0 else inner[::-1])]
    return [row * columns + column for row, column in order]


def cost(flops, moved, part=64):
    return pl.CostEstimate(flops=flops // part, bytes_accessed=moved // part, transcendentals=0)


def ordered_rows(axis, features, order):
    rows = features.shape[0]
    place = lax.broadcasted_iota(jnp.int32, (rows, rows), 0) + lax.axis_index(axis) * rows
    chosen = (place == order[...]).astype(jnp.bfloat16)
    return lax.dot_general(
        chosen, features[...], (((0,), (0,)), ((), ())), preferred_element_type=jnp.float32
    )


def norm_kernel(axis, features, order, gain, normed, *parts):
    picked = ordered_rows(axis, features, order)
    factor = lax.rsqrt(jnp.mean(picked * picked, axis=-1, keepdims=True) + EPS)
    found = (picked * factor * gain[...]).astype(jnp.bfloat16)
    normed[...] = found
    size = found.shape[0] // len(parts)
    for index, part in enumerate(parts):
        part[...] = found[index * size : (index + 1) * size]


def prepare(features, order, gain):
    rows, width = features.shape
    half = jax.ShapeDtypeStruct((rows // 2, width), jnp.bfloat16)
    return pl.pallas_call(
        functools.partial(norm_kernel, "seq"),
        out_shape=[jax.ShapeDtypeStruct((rows, width), jnp.bfloat16), half, half],
        compiler_params=pltpu.CompilerParams(vmem_limit_bytes=16 * MIB),
        cost_estimate=cost(2 * rows * rows * width, 6 * rows * width),
        name="norm",
    )(features, order, gain.reshape(1, width))


def choose_kernel(axis, one, other, chosen, arrived):
    straight = lax.axis_index(axis) == 0

    @pl.when(straight)
    def _():
        pltpu.make_async_copy(one, chosen, arrived).start()

    @pl.when(jnp.logical_not(straight))
    def _():
        pltpu.make_async_copy(other, chosen, arrived).start()

    pltpu.make_async_copy(one, chosen, arrived).wait()


def choose(axis, one, other, limit):
    anywhere = pl.BlockSpec(memory_space=pl.ANY)
    return pl.pallas_call(
        functools.partial(choose_kernel, axis),
        out_shape=jax.ShapeDtypeStruct(one.shape, one.dtype),
        in_specs=[anywhere, anywhere],
        out_specs=pl.BlockSpec(memory_space=pltpu.VMEM),
        scratch_shapes=[pltpu.SemaphoreType.DMA],
        compiler_params=pltpu.CompilerParams(vmem_limit_bytes=limit * MIB),
        cost_estimate=cost(0, 6 * one.size),
        name="choose",
    )(one, other)


def head_scale(values, head_dim, gain):
    columns = values.shape[1]
    row = lax.broadcasted_iota(jnp.int32, (columns, columns), 0) // head_dim
    column = lax.broadcasted_iota(jnp.int32, (columns, columns), 1) // head_dim
    same = (row == column).astype(jnp.bfloat16)
    sums = jnp.dot(
        (values * values).astype(jnp.bfloat16), same, preferred_element_type=jnp.float32
    )
    factor = lax.rsqrt(sums * (1.0 / head_dim) + EPS)
    return (values * factor * gain).astype(jnp.bfloat16)


def project_into(source, weights, first, head_dim, scaled, out):
    width = source.shape[1]
    chunk = 4 * head_dim
    at = 0
    for columns, gain in scaled:
        for _ in range(columns // chunk):
            found = jnp.dot(
                source, weights[:, first + at : first + at + chunk],
                preferred_element_type=jnp.float32,
            )
            out(at, found.astype(jnp.bfloat16) if gain is None else head_scale(found, head_dim, gain))
            at += chunk


def project_into(source, weights, first, head_dim, scaled, out):
    width = source.shape[1]
    chunk = 4 * head_dim
    at = 0
    for columns, gain in scaled:
        for _ in range(columns // chunk):
            found = jnp.dot(
                source, weights[:, first + at : first + at + chunk],
                preferred_element_type=jnp.float32,
            )
            out(at, found.astype(jnp.bfloat16) if gain is None else head_scale(found, head_dim, gain))
            at += chunk


def project_kernel(axis, head_dim, scale, count, with_queries, *refs):
    if with_queries:
        features, order, *refs, ordered, key_values, gathered = refs
        ordered[...] = ordered_rows(axis, features, order).astype(jnp.bfloat16)
        refs = [*refs, key_values, gathered]
    sources = refs[:count]
    weights, query_gain, key_gain, *rest = refs[count:]
    queries = rest[0] if with_queries else None
    key_values, gathered = rest[-2:]
    width = sources[0].shape[1]
    chunk = 4 * head_dim
    at = 0
    for source in sources:
        gathered[at : at + source.shape[0], :] = source[...]
        at += source.shape[0]

    def store_key_value(at, value):
        key_values[:, at : at + chunk] = value

    def store_query(at, value):
        queries[:, at : at + chunk] = value

    if with_queries:
        gain = query_gain[...] * scale
        project_into(sources[0][...], weights, 0, head_dim, [(width, gain)], store_query)
    project_into(
        gathered[...], weights, width, head_dim, [(width, key_gain[...]), (width, None)],
        store_key_value,
    )


def project(sources, weights, query_gain, key_gain, unordered=()):
    with_queries = bool(unordered)
    width = sources[0].shape[1]
    rows = sum(source.shape[0] for source in sources)
    head_dim = query_gain.shape[0]
    shapes = [jax.ShapeDtypeStruct((rows, 2 * width), jnp.bfloat16)]
    if with_queries:
        shapes = [jax.ShapeDtypeStruct(sources[0].shape, jnp.bfloat16)] * 2 + shapes
    local = pl.BlockSpec(memory_space=pltpu.VMEM)
    return pl.pallas_call(
        functools.partial(
            project_kernel, "seq", head_dim, 2.0 / math.sqrt(head_dim), len(sources), with_queries
        ),
        out_shape=shapes,
        in_specs=[local] * (len(unordered) + len(sources) + 3),
        out_specs=[local] * len(shapes),
        scratch_shapes=[pltpu.VMEM((rows, width), jnp.bfloat16)],
        compiler_params=pltpu.CompilerParams(vmem_limit_bytes=24 * MIB),
        cost_estimate=cost(4 * rows * width * width, 8 * width * width),
        name="project",
    )(*unordered, *sources, weights, jnp.tile(query_gain, 4)[None], jnp.tile(key_gain, 4)[None])


def slot_of(block, me, cycle, blocks):
    holder = lax.div(block, blocks)
    away = lax.rem(holder - me + REACH + cycle, cycle) - REACH
    turned = away * (1 - 2 * lax.rem(me, 2))
    return jnp.where(turned > 0, 2 * turned - 1, -2 * turned), lax.rem(block, blocks)


def pick_blocks(lists, counts, picks, at, me, cycle, blocks, wanted):
    found = 0
    count = counts[at]
    for index in range(MAXNZ):
        slot, place = slot_of(lists[at, index], me, cycle, blocks)
        take = (index < count) & wanted(slot)
        spot = found

        @pl.when(take)
        def _(slot=slot, place=place, spot=spot):
            picks[spot] = slot * blocks + place

        found = found + take.astype(jnp.int32)

    @pl.when(lax.rem(found, 2) == 1)
    def _(found=found):
        picks[found] = picks[found - 1]

    return found


def add_blocks(queries, window, picks, sums, here, count):
    width = queries.shape[1]
    pairs = sums.shape[0]
    pair = width // pairs
    low = lax.broadcasted_iota(jnp.int32, (BLOCK, pair), 1) < pair // 2
    key_lane = lax.broadcasted_iota(jnp.int32, (2 * BLOCK, 2 * BLOCK), 1)
    ones = jnp.ones((2 * BLOCK, pair), jnp.bfloat16)

    def two_blocks(step, carry):
        one = pl.ds(pl.multiple_of(picks[2 * step] * BLOCK, BLOCK), BLOCK)
        other = pl.ds(pl.multiple_of(picks[2 * step + 1] * BLOCK, BLOCK), BLOCK)
        kept = key_lane < jnp.where(2 * step + 1 < count, 2 * BLOCK, BLOCK)
        for index in range(pairs):
            columns = pl.ds(index * pair, pair)
            later = pl.ds(width + index * pair, pair)
            asked = queries[here, columns]
            none = jnp.zeros_like(asked)
            both = jnp.concatenate(
                [jnp.where(low, asked, none), jnp.where(low, none, asked)], axis=0
            )
            known = jnp.concatenate([window[one, columns], window[other, columns]], axis=0)
            held = jnp.concatenate([window[one, later], window[other, later]], axis=0)
            scores = lax.dot_general(
                both, known, (((1,), (1,)), ((), ())), preferred_element_type=jnp.float32
            )
            shares = jnp.where(kept, jnp.exp(scores), 0.0).astype(jnp.bfloat16)
            found = jnp.dot(
                shares, jnp.concatenate([held, ones], axis=1), preferred_element_type=jnp.float32
            )
            sums[index] = jnp.where(step == 0, found, sums[index] + found)
        return carry

    lax.fori_loop(0, lax.div(count + 1, 2), two_blocks, 0)


def attend_kernel(
    axis, cycle, lists, counts, queries, own_mate, near, across, mixed, totals,
    sums, window, picks,
):
    rows, width = queries.shape
    blocks = rows // BLOCK
    pairs = sums.shape[0]
    pair = width // pairs
    me = lax.axis_index(axis)
    low = lax.broadcasted_iota(jnp.int32, (BLOCK, pair), 1) < pair // 2
    window[: 2 * rows, :] = own_mate[...]
    window[2 * rows : 3 * rows, :] = near[...]
    window[3 * rows :, :] = across[...]
    for at in range(blocks):
        here = pl.ds(at * BLOCK, BLOCK)
        count = pick_blocks(
            lists, counts, picks, at, me, cycle, blocks, lambda slot: slot < 2 * REACH
        )
        add_blocks(queries, window, picks, sums, here, count)
        for index in range(pairs):
            total = sums[index]
            columns = pl.ds(index * pair, pair)
            mixed[here, columns] = jnp.where(low, total[:BLOCK, :pair], total[BLOCK:, :pair])
            totals[here, columns] = jnp.where(low, total[:BLOCK, pair:], total[BLOCK:, pair:])


def attend(axis, cycle, lists, counts, queries, sources):
    rows, width = queries.shape
    shape = jax.ShapeDtypeStruct((rows, width), jnp.float32)
    scalars = pl.BlockSpec(memory_space=pltpu.SMEM)
    local = pl.BlockSpec(memory_space=pltpu.VMEM)
    pairs = width // BLOCK
    slots = 2 * REACH
    work = 2 * rows * MAXNZ * BLOCK * width
    return pl.pallas_call(
        functools.partial(attend_kernel, axis, cycle),
        out_shape=(shape, shape),
        in_specs=[scalars, scalars, local] + [local] * len(sources),
        out_specs=(local, local),
        scratch_shapes=[
            pltpu.VMEM((pairs, 2 * BLOCK, 2 * BLOCK), jnp.float32),
            pltpu.VMEM((slots * rows, 2 * width), jnp.bfloat16),
            pltpu.SMEM((MAXNZ,), jnp.int32),
        ],
        compiler_params=pltpu.CompilerParams(vmem_limit_bytes=32 * MIB),
        cost_estimate=pl.CostEstimate(
            flops=ATTEND_COST, bytes_accessed=4 * slots * rows * width, transcendentals=0
        ),
        name="attend",
    )(lists, counts, queries, *sources)


def finish_kernel(
    axis, cycle, lists, counts, queries, window, mixed, totals, attention, sums, picks,
):
    rows, width = queries.shape
    blocks = rows // BLOCK
    pairs = sums.shape[0]
    pair = width // pairs
    me = lax.axis_index(axis)
    low = lax.broadcasted_iota(jnp.int32, (BLOCK, pair), 1) < pair // 2

    for at in range(blocks):
        here = pl.ds(at * BLOCK, BLOCK)
        count = pick_blocks(
            lists, counts, picks, at, me, cycle, blocks, lambda slot: slot == 2 * REACH
        )
        shift = 2 * REACH * blocks

        @pl.when(count == 0)
        def _():
            sums[...] = jnp.zeros_like(sums)

        for index in range(blocks + 1):
            picks[index] = jnp.clip(picks[index] - shift, 0, blocks - 1)
        add_blocks(queries, window, picks, sums, here, count)
        for index in range(pairs):
            total = sums[index]
            columns = pl.ds(index * pair, pair)
            share = (
                mixed[here, columns] + jnp.where(low, total[:BLOCK, :pair], total[BLOCK:, :pair])
            ) / (
                totals[here, columns] + jnp.where(low, total[:BLOCK, pair:], total[BLOCK:, pair:])
            )
            attention[here, columns] = share.astype(jnp.bfloat16)


def finish(
    axis, cycle, lists, counts, queries, far_kv, mixed, totals
):
    rows, width = queries.shape
    shape = jax.ShapeDtypeStruct((rows, width), jnp.bfloat16)
    scalars = pl.BlockSpec(memory_space=pltpu.SMEM)
    local = pl.BlockSpec(memory_space=pltpu.VMEM)
    pairs = width // BLOCK
    return pl.pallas_call(
        functools.partial(finish_kernel, axis, cycle),
        out_shape=shape,
        in_specs=[scalars, scalars] + [local] * 4,
        out_specs=local,
        scratch_shapes=[
            pltpu.VMEM((pairs, 2 * BLOCK, 2 * BLOCK), jnp.float32),
            pltpu.SMEM((MAXNZ,), jnp.int32),
        ],
        compiler_params=pltpu.CompilerParams(vmem_limit_bytes=32 * MIB),
        cost_estimate=cost(6 * rows * width * width, 8 * width * width),
        name="finish",
    )(
        lists, counts, queries, far_kv, mixed, totals
    )


def output_kernel(attention, ordered, weights, gain, attended, *seconds):
    product = jnp.dot(attention[...], weights[...], preferred_element_type=jnp.float32)
    result = (ordered[...].astype(jnp.float32) + product).astype(jnp.bfloat16)
    attended[...] = result
    widened = result.astype(jnp.float32)
    factor = lax.rsqrt(jnp.mean(widened * widened, axis=-1, keepdims=True) + EPS)
    second = (widened * factor * gain[...]).astype(jnp.bfloat16)
    part = second.shape[0] // len(seconds)
    for index, kept in enumerate(seconds):
        kept[...] = second[index * part : (index + 1) * part]


def attention_output(attention, ordered, weights, gain, parts):
    rows, width = attention.shape
    shape = jax.ShapeDtypeStruct((rows, width), jnp.bfloat16)
    return pl.pallas_call(
        output_kernel,
        out_shape=[shape] + [jax.ShapeDtypeStruct((rows // parts, width), jnp.bfloat16)] * parts,
        compiler_params=pltpu.CompilerParams(vmem_limit_bytes=24 * MIB),
        cost_estimate=cost(2 * rows * width * width, 2 * width * width),
        name="attention_output",
    )(attention, ordered, weights, gain.reshape(1, width))


def pieces_kernel(axis, swaps, sources, bases, has_known, *refs):
    count = len(swaps)
    seconds, refs = refs[:sources], refs[sources:]
    firsts, refs = refs[:count], refs[count:]
    lasts, refs = refs[:count], refs[count:]
    base, refs = refs[:bases], refs[bases:]
    known, results = (refs[0], refs[1:]) if has_known else (None, refs)
    straight = lax.axis_index(axis) == 0
    rows = jnp.concatenate([second[...] for second in seconds], axis=0)
    total = None
    for index, swapped in enumerate(swaps):
        first_rows, last_rows = firsts[index][...], lasts[index][...]
        if swapped:
            first_rows, last_rows = (
                jnp.where(straight, first_rows, last_rows),
                jnp.where(straight, last_rows, first_rows),
            )
        before = lax.dot_general(
            rows, first_rows, (((1,), (1,)), ((), ())), preferred_element_type=jnp.float32
        )
        active = jax.nn.gelu(before, approximate=True).astype(jnp.bfloat16)
        part = jnp.dot(active, last_rows, preferred_element_type=jnp.float32)
        total = part if total is None else total + part
    if bases:
        total = total + jnp.concatenate([part[...] for part in base], axis=0).astype(jnp.float32)
    if has_known:
        total = total + known[...]
    part = total.shape[0] // len(results)
    for index, result in enumerate(results):
        result[...] = total[index * part : (index + 1) * part].astype(result.dtype)


def feed_pieces(axis, seconds, pieces, base, dtype, parts=1, known=None):
    rows = sum(second.shape[0] for second in seconds)
    width = seconds[0].shape[1]
    hidden = sum(piece[0].shape[0] for piece in pieces)
    operands = [*seconds] + [piece[0] for piece in pieces] + [piece[1] for piece in pieces]
    return pl.pallas_call(
        functools.partial(
            pieces_kernel, axis, tuple(piece[2] for piece in pieces), len(seconds), len(base),
            known is not None,
        ),
        out_shape=[jax.ShapeDtypeStruct((rows // parts, width), dtype)] * parts,
        compiler_params=pltpu.CompilerParams(vmem_limit_bytes=24 * MIB),
        cost_estimate=cost(4 * rows * width * hidden, 4 * hidden * width),
        name="feed_pieces",
    )(*operands, *base, *([] if known is None else [known]))


def total_kernel(attended, own, *refs):
    *returned, result = refs
    part = result.shape[0] // len(returned)
    for index, back in enumerate(returned):
        here = pl.ds(index * part, part)
        result[here, :] = (
            attended[here, :].astype(jnp.float32) + own[here, :] + back[...].astype(jnp.float32)
        ).astype(result.dtype)


def total_of(attended, own, returned):
    return pl.pallas_call(
        total_kernel,
        out_shape=jax.ShapeDtypeStruct(attended.shape, attended.dtype),
        compiler_params=pltpu.CompilerParams(vmem_limit_bytes=16 * MIB),
        cost_estimate=cost(attended.size, 10 * attended.size),
        name="total",
    )(attended, own, *returned)


def feed_kernel(steps, second, first_rows, second_rows, attended, result, total):
    step = pl.program_id(0)
    before = lax.dot_general(
        second[...], first_rows[...], (((1,), (1,)), ((), ())), preferred_element_type=jnp.float32
    )
    active = jax.nn.gelu(before, approximate=True).astype(jnp.bfloat16)
    part = jnp.dot(active, second_rows[...], preferred_element_type=jnp.float32)

    @pl.when(step == 0)
    def _():
        total[...] = part

    @pl.when(step > 0)
    def _():
        total[...] += part

    @pl.when(step == steps - 1)
    def _():
        result[...] = (attended[...].astype(jnp.float32) + total[...]).astype(jnp.bfloat16)


def feed_forward(second, first_rows, second_rows, attended):
    rows, width = second.shape
    hidden = first_rows.shape[0]
    chunk = min(512, hidden)
    steps = hidden // chunk
    whole = pl.BlockSpec((rows, width), lambda i: (0, 0))
    part = pl.BlockSpec((chunk, width), lambda i: (i, 0))
    return pl.pallas_call(
        functools.partial(feed_kernel, steps),
        out_shape=jax.ShapeDtypeStruct((rows, width), jnp.bfloat16),
        grid=(steps,),
        in_specs=[whole, part, part, whole],
        out_specs=whole,
        scratch_shapes=[pltpu.VMEM((rows, width), jnp.float32)],
        compiler_params=pltpu.CompilerParams(vmem_limit_bytes=40 * MIB),
        cost_estimate=pl.CostEstimate(
            flops=4 * rows * width * hidden,
            bytes_accessed=4 * hidden * width + 6 * rows * width,
            transcendentals=rows * hidden,
        ),
        name="feed_forward",
    )(second, first_rows, second_rows, attended)


def shards(
    pore_features,
    pore_order,
    block_lists,
    block_counts,
    norm1_gain,
    w_qkv,
    query_gain,
    key_gain,
    w_attn_out,
    norm2_gain,
    w_in,
    w_out,
):
    rows = pore_features.shape[0]
    cycle = lax.axis_size("seq")
    me = lax.axis_index("seq")

    def moved(value, where):
        return lax.ppermute(value, "seq", [(i, where(i) % cycle) for i in range(cycle)])

    def mate_of(value):
        return moved(value, lambda i: i + 1 - 2 * (i % 2))

    chip_rows, chip_columns = chip_grid(cycle // 2)
    lane = 2 * chip_columns

    def along(value, targets):
        pairs = [(lane * a + k, lane * b + k) for a, b in targets for k in range(lane)]
        return lax.ppermute(value, "seq", pairs)

    def beside(value):
        return moved(value, lambda i: i + 2 - 4 * (i // 2 % 2))

    def over(value):
        return lax.ppermute(value, "parts", [(0, 1), (1, 0)])

    shared = (chip_rows, chip_columns) == (4, 2) and lax.axis_size("parts") == 2
    if shared:
        swap = [(0, 1), (1, 0), (2, 3), (3, 2)]
        prime = choose("parts", w_in, w_out, 60)
        pair_rows = along(prime, swap)
        third = along(prime, [(0, 2), (1, 3), (2, 0), (3, 1)])
    order = pore_order.reshape(1, rows)
    normed, *normed_parts = prepare(pore_features, order, norm1_gain)
    near = [moved(part, lambda i: i - 1 + 2 * (i % 2)) for part in normed_parts]
    mate = mate_of(normed)
    queries, ordered, own_mate = project(
        [normed, mate], w_qkv, query_gain, key_gain, (pore_features, order)
    )
    queries, late_normed, *near = lax.optimization_barrier((queries, normed, *near))
    far = moved(late_normed, lambda i: i + 2 - 4 * (i % 2))
    across = [mate_of(piece) for part in near for piece in jnp.split(part, 2)]

    (near_kv,) = project(near, w_qkv, query_gain, key_gain)
    if shared:
        left = choose("parts", w_out, w_in, 8)
        near_kv, left, *across = lax.optimization_barrier((near_kv, left, *across))
    (across_kv,) = project(across, w_qkv, query_gain, key_gain)
    mixed, totals = attend(
        "seq", cycle, block_lists, block_counts, queries, [own_mate, near_kv, across_kv]
    )
    if shared:
        mixed, totals, third, pair_rows, left = lax.optimization_barrier(
            (mixed, totals, third, pair_rows, left)
        )
        other_pair = along(left, swap)
        fourth = along(third, swap)
        other_third = over(third)
        mixed, totals, far = lax.optimization_barrier((mixed, totals, far))
    (far_kv,) = project([far], w_qkv, query_gain, key_gain)
    attention = finish(
        "seq", cycle, block_lists, block_counts, queries, far_kv, mixed, totals
    )
    parts = 2 if shared else 1
    attended, *seconds = attention_output(attention, ordered, w_attn_out, norm2_gain, parts)
    if shared:
        guests = [beside(second) for second in seconds]
        mate_seconds = [mate_of(second) for second in seconds]
        attended, fourth = lax.optimization_barrier((attended, fourth))
        guests[0], other_pair, other_third = lax.optimization_barrier(
            (guests[0], other_pair, other_third)
        )
        other_fourth = over(fourth)
        pieces = [
            (w_in, w_out, False),
            (pair_rows, other_pair, True),
            (third, other_third, True),
        ]
        guest_mate_parts = []
        guest_parts = []
        for index in range(parts):
            guest_mate_parts += feed_pieces(
                "parts", [mate_of(part) for part in jnp.split(guests[index], 2)], pieces, [], jnp.bfloat16
            )
            guest_parts += feed_pieces("parts", [guests[index]], pieces, [], jnp.float32)
            if index == 0:
                guests[1], guest_mate_parts[0], guest_parts[0], other_fourth = (
                    lax.optimization_barrier(
                        (guests[1], guest_mate_parts[0], guest_parts[0], other_fourth)
                    )
                )
        last = [
            (fourth, other_fourth, True),
            (mate_of(fourth), mate_of(other_fourth), True),
        ]
        returned = []
        for guest, part, base in zip(guests, guest_parts, guest_mate_parts):
            (guest_part,) = feed_pieces(
                "parts", [guest], last, [mate_of(base)], jnp.bfloat16, 1, part
            )
            returned.append(beside(guest_part))
        mate_parts = feed_pieces("parts", mate_seconds, pieces, [], jnp.bfloat16, 4)
        (own_main,) = feed_pieces("parts", seconds, pieces, [], jnp.float32)
        returned[0], own_main = lax.optimization_barrier((returned[0], own_main))
        (own_part,) = feed_pieces(
            "parts", seconds, last, [mate_of(part) for part in mate_parts], jnp.float32, 1, own_main
        )
        layer_output = total_of(attended, own_part, returned)
    else:
        ring = [2 * chip + core for chip in chip_cycle(cycle // 2) for core in range(2)]
        gathered_in = lax.all_gather(w_in, "seq", axis=0, tiled=True, axis_index_groups=[ring])
        gathered_out = lax.all_gather(w_out, "seq", axis=0, tiled=True, axis_index_groups=[ring])
        layer_output = feed_forward(seconds[0], gathered_in, gathered_out, attended)
    return (attended, layer_output)


def solution(mesh):
    return jax.shard_map(
        shards,
        mesh=mesh,
        in_specs=(
            P(("parts", "seq"), None),
            P(("parts", "seq")),
            P(("parts", "seq"), None),
            P(("parts", "seq")),
            P(),
            P(),
            P(),
            P(),
            P(),
            P(),
            P("seq", None),
            P("seq", None),
        ),
        out_specs=(P(("parts", "seq"), None), P(("parts", "seq"), None)),
        check_vma=False,
    )
```
